512 devices in a mesh: dp: 512 (over z, x, y, core).
Axes of the slice: x: 4, y: 4, z: 16, core: 2. Of those that a mesh axis runs over, the one named last changes fastest.
Arguments:
- queries: bfloat16 [16384, 32, 128], P('dp'), may hold values from -10 to 10
- positives: int32 [16384], P('dp'), may hold values from 0 to 3
- pages: bfloat16 [512, 1024, 128], P('dp'), may hold values from -1.5 to 1.5
Outputs:
- loss: float32 [16384], P('dp')
- query_grad: float32 [16384, 32, 128], P('dp')
- page_grad: float32 [512, 1024, 128], P('dp')
The draws below stay inside these ranges and needn't reach their ends.
All inputs are finite; a program needn't handle non-finite values.
Results may differ from the reference program's by a relative error of at most 0.0059.
Values may be sent and summed in bfloat16 or wider, within the bound.
No kernel may reach another device: no remote copies, remote signals or barrier semaphores. Data moves between devices by JAX's collectives and lax.ppermute only.
A program may use at most 64 MiB of HBM per device.

```python
import math
import jax
import jax.numpy as jnp
from jax import lax

D = 128
QT = 32
P_SIZE = 1024
W = 4
Q_DEV = 32
QUERIES = 16384
PAGES = 512
N_DP = 512


def base_pages(key):
    spread = 2.0 / math.sqrt(D)
    cut = min(6.0, 0.55 * math.sqrt(D))
    varying = spread * jax.random.truncated_normal(key, -cut, cut, (PAGES, P_SIZE, D), jnp.float32)
    centre = 0.12 * jax.random.truncated_normal(jax.random.fold_in(key, 11), -3.0, 3.0, (PAGES, 1, D), jnp.float32)
    return varying + centre


def draw_pages(key, part):
    values = base_pages(key)
    return values.astype(jnp.bfloat16)


def draw_queries(key, part):
    key = jax.random.fold_in(key, 3)
    shared = 0.04 * jax.random.truncated_normal(jax.random.fold_in(key, 1), -4.0, 4.0, (QUERIES, 1, D), jnp.float32)
    noise = 0.03 * jax.random.truncated_normal(key, -6.0, 6.0, (QUERIES, QT, D), jnp.float32)
    values = shared + noise
    return values.astype(jnp.bfloat16)


def with_ends(result, own_key, low, high):
    longest = result.shape.index(max(result.shape))
    spots = []
    for shift in (0, 1):
        where = [jax.random.randint(jax.random.fold_in(own_key, axis), (), 0, length) for axis, length in enumerate(result.shape)]
        where[longest] = (where[longest] + shift) % result.shape[longest]
        spots.append(tuple(where))
    return result.at[spots[0]].set(low).at[spots[1]].set(high)


def setup_inputs(seed: int = 0) -> dict:
    seeds = jax.random.split(jax.random.key(seed), 4)
    return {
        "queries": draw_queries(jax.random.fold_in(seeds[3], 71), 0),
        "positives": with_ends(jax.random.randint(seeds[1], (QUERIES,), 0, W), jax.random.fold_in(seeds[1], 1), 0, W - 1).astype(jnp.int32),
        "pages": draw_pages(jax.random.fold_in(seeds[3], 71), 0),
    }


tau_scale = 0.1


def token_scores(query_rows, page):
    logits = lax.dot_general(query_rows, page, (((1,), (1,)), ((), ())), preferred_element_type=jnp.float32) / tau_scale
    largest = jnp.max(logits, axis=1, keepdims=True)
    powers = jnp.exp(logits - largest)
    total = jnp.sum(powers, axis=1, keepdims=True)
    return powers, total, largest


def device_terms(query_block, positive, window):
    count, tokens, width = query_block.shape
    query_rows = query_block.reshape(count * tokens, width)
    score_list = []
    kept = []
    for page in window:
        powers, total, largest = token_scores(query_rows, page)
        kept.append((powers, total))
        smooth_max = tau_scale * (largest[:, 0] + jnp.log(total[:, 0]))
        score_list.append(jnp.sum(smooth_max.reshape(count, tokens), axis=1))
    scores = jnp.stack(score_list, axis=1)
    is_positive = (jnp.arange(len(window), dtype=jnp.int32)[None, :] == positive[:, None]).astype(jnp.float32)
    positive_score = jnp.sum(is_positive * scores, axis=1, keepdims=True)
    margins = scores - positive_score
    others = 1.0 - is_positive
    loss = jnp.sum(others * jax.nn.softplus(margins), axis=1)
    sigmoid_terms = others * jax.nn.sigmoid(margins)
    slopes = sigmoid_terms - is_positive * jnp.sum(sigmoid_terms, axis=1, keepdims=True)
    query_grad = jnp.zeros((count * tokens, width), jnp.float32)
    page_terms = []
    for offset, page in enumerate(window):
        powers, total = kept[offset]
        row_slope = jnp.repeat(slopes[:, offset], tokens)[:, None]
        weight = (powers * (row_slope / total)).astype(jnp.bfloat16)
        query_grad = query_grad + jnp.dot(weight, page, preferred_element_type=jnp.float32)
        page_terms.append(lax.dot_general(weight, query_rows, (((0,), (0,)), ((), ())), preferred_element_type=jnp.float32))
    return loss, query_grad.reshape(count, tokens, width), page_terms


def reference(queries, positives, pages):
    query_sets = queries.reshape(N_DP, Q_DEV, QT, D)
    positive_sets = positives.reshape(N_DP, Q_DEV)

    def one_device(grad_total, device):
        query_block = lax.dynamic_index_in_dim(query_sets, device, 0, keepdims=False)
        positive = lax.dynamic_index_in_dim(positive_sets, device, 0, keepdims=False)
        owners = [((device - offset) % N_DP).astype(jnp.int32) for offset in range(W)]
        window = [lax.dynamic_index_in_dim(pages, owner, 0, keepdims=False) for owner in owners]
        loss, query_grad, page_terms = device_terms(query_block, positive, window)
        for owner, term in zip(owners, page_terms):
            current = lax.dynamic_index_in_dim(grad_total, owner, 0, keepdims=False)
            grad_total = lax.dynamic_update_index_in_dim(grad_total, current + term, owner, 0)
        return grad_total, (loss, query_grad)

    start = jnp.zeros((N_DP, P_SIZE, D), jnp.float32)
    page_grad, (loss, query_grad) = lax.scan(one_device, start, jnp.arange(N_DP, dtype=jnp.int32))
    return loss.reshape(QUERIES), query_grad.reshape(QUERIES, QT, D), page_grad
```

```python
import functools
import math

import jax
import jax.numpy as jnp
from jax import lax
from jax.experimental import pallas as pl
from jax.experimental.pallas import tpu as pltpu
from jax.sharding import PartitionSpec as P


tau_scale = 0.1
EXPONENT = math.log2(math.e) / tau_scale
CHUNK = 256
PAD = 16
MIB = 1024 * 1024

VMEM = pl.BlockSpec(memory_space=pltpu.VMEM)


def passed_along(value, axis, steps):
    count = lax.axis_size(axis)
    pairs = [(source, (source + steps) % count) for source in range(count)]
    return lax.ppermute(value, axis, pairs)


def on_core(body, outs, args, flops, name, limit=24):
    return pl.pallas_call(
        body,
        out_shape=[pltpu.VMEM(shape, dtype) for shape, dtype in outs],
        in_specs=[VMEM] * len(args),
        out_specs=[VMEM] * len(outs),
        compiler_params=pltpu.CompilerParams(vmem_limit_bytes=limit * MIB),
        cost_estimate=pl.CostEstimate(flops=flops, bytes_accessed=2 * MIB, transcendentals=0),
        name=name,
    )(*args)


def rows_dot(a, b):
    return lax.dot_general(a, b, (((1,), (1,)), ((), ())), preferred_element_type=jnp.float32)


def token_powers(page, query, powers_ref, total_ref, smooth_ref, row):
    rows = query.shape[0]
    for start in range(0, rows, CHUNK):
        cut = slice(start, start + CHUNK)
        products = rows_dot(page[...], query[cut, :])
        largest = jnp.max(products, axis=0, keepdims=True)
        powers = jnp.exp2((products - largest) * EXPONENT)
        total = jnp.sum(powers, axis=0, keepdims=True)
        powers_ref[:, cut] = powers.astype(jnp.bfloat16)
        total_ref[row : row + 1, cut] = total
        smooth_ref[row : row + 1, cut] = largest + tau_scale * jnp.log(total)


def mix_pages(page_t, powers_ref, mixed_ref):
    rows = powers_ref.shape[1]
    for start in range(0, rows, CHUNK):
        cut = slice(start, start + CHUNK)
        mixed_ref[:, cut] = jnp.dot(page_t, powers_ref[:, cut], preferred_element_type=jnp.float32)


def turned(value):
    return value.astype(jnp.float32).T.astype(jnp.bfloat16)


def unit_body(page, query, powers_ref, mixed_ref, total_ref, smooth_ref, query_t_ref):
    token_powers(page, query, powers_ref, total_ref, smooth_ref, 0)
    mix_pages(turned(page[...]), powers_ref, mixed_ref)
    query_t_ref[...] = turned(query[...])


def query_sums(value, tokens):
    lane = lax.broadcasted_iota(jnp.int32, value.shape, 1)
    width = value.shape[1]
    step = tokens // 2
    while step:
        ahead = pltpu.roll(value, width - step, 1)
        behind = pltpu.roll(value, step, 1)
        value = value + jnp.where((lane & step) != 0, behind, ahead)
        step //= 2
    return value


def pair_body(tokens, page, query, next_query, smooth_a, smooth_b, positive,
              powers_a_ref, powers_b_ref, total_ref, own_ref, next_ref, smooth_ref):
    token_powers(page, query, powers_a_ref, total_ref, smooth_ref, 0)
    token_powers(page, next_query, powers_b_ref, total_ref, smooth_ref, 1)
    rows = jnp.concatenate([smooth_a[...], smooth_ref[0:1, :], smooth_b[...], smooth_ref[1:2, :]], axis=0)
    sums = query_sums(rows, tokens)
    own_ref[0:2, :] = sums[0:2, :]
    own_ref[2:3, :] = positive[...]
    own_ref[3:4, :] = positive[...]
    next_ref[...] = sums[2:4, :]


def mix_body(page, powers_a, powers_b, mixed_a_ref, mixed_b_ref):
    page_t = turned(page[...])
    mix_pages(page_t, powers_a, mixed_a_ref)
    mix_pages(page_t, powers_b, mixed_b_ref)


def slopes_of(scores, positive):
    flags = [(positive == float(offset)).astype(jnp.float32) for offset in range(4)]
    positive_score = sum(flag * score for flag, score in zip(flags, scores))
    margins = [score - positive_score for score in scores]
    loss = sum((1.0 - flag) * jax.nn.softplus(margin) for flag, margin in zip(flags, margins))
    terms = [(1.0 - flag) * jax.nn.sigmoid(margin) for flag, margin in zip(flags, margins)]
    total = sum(terms)
    return loss, [term - flag * total for flag, term in zip(flags, terms)]


def to_short(value):
    largest = jnp.maximum(jnp.max(jnp.abs(value), axis=0, keepdims=True), 1e-38)
    power = jnp.minimum(jnp.floor(math.log2(32000.0) - jnp.log2(largest)), 126.0)
    short = jnp.round(value * jnp.exp2(power)).astype(jnp.int32).astype(jnp.int16)
    tail = jnp.broadcast_to(power, (PAD, value.shape[1])).astype(jnp.int32).astype(jnp.int16)
    return short, tail


def from_short(ref, rows):
    power = ref[rows : rows + PAD, :].astype(jnp.int32).astype(jnp.float32)[0:1, :]
    return ref[0:rows, :].astype(jnp.int32).astype(jnp.float32) * jnp.exp2(-power)


def scaled(query_t, weight):
    return (query_t.astype(jnp.float32) * weight).astype(jnp.bfloat16)


def send_body(from_next, from_last, own, onward, total_own_a, total_own_b, total_far, query_t, next_query_t,
              powers_a, powers_b, mixed_own_b, mixed_far_b,
              page_out_ref, query_out_ref, loss_ref, weight_ref):
    loss, slopes = slopes_of([own[0:1, :], from_last[0:1, :], own[1:2, :], from_last[1:2, :]], own[2:3, :])
    _, next_slopes = slopes_of([from_next[0:1, :], onward[0:1, :], from_next[1:2, :], onward[1:2, :]], from_next[2:3, :])
    loss_ref[...] = loss
    weight_own_a = slopes[0] / total_own_a[...]
    weight_far_a = slopes[2] / total_far[0:1, :]
    weight_own_b = next_slopes[1] / total_own_b[...]
    weight_far_b = next_slopes[3] / total_far[1:2, :]
    weight_ref[0:1, :] = weight_own_a
    weight_ref[1:2, :] = weight_own_b
    weight_ref[2:3, :] = weight_far_a
    weight_ref[3:4, :] = weight_far_b
    page_term = rows_dot(powers_a[...], scaled(query_t[...], weight_far_a))
    page_term = page_term + rows_dot(powers_b[...], scaled(next_query_t[...], weight_far_b))
    count = page_term.shape[0]
    short, tail = to_short(page_term)
    page_out_ref[0:count, :] = short
    page_out_ref[count : count + PAD, :] = tail
    query_term = mixed_own_b[...] * weight_own_b + mixed_far_b[...] * weight_far_b
    width = query_term.shape[0]
    short, tail = to_short(query_term)
    query_out_ref[0:width, :] = short
    query_out_ref[width : width + PAD, :] = tail


def keep_body(weight, query_t, next_query_t, powers_a, powers_b, mixed_own_a, mixed_far_a,
              page_ref, query_ref):
    page_term = rows_dot(powers_a[...], scaled(query_t[...], weight[0:1, :]))
    page_ref[...] = page_term + rows_dot(powers_b[...], scaled(next_query_t[...], weight[1:2, :]))
    query_ref[...] = mixed_own_a[...] * weight[0:1, :] + mixed_far_a[...] * weight[2:3, :]


def last_body(page_own, query_own, page_in, query_in, page_ref, query_ref):
    query_ref[...] = (query_own[...] + from_short(query_in, query_own.shape[0])).T
    page_ref[...] = page_own[...] + from_short(page_in, page_own.shape[0])


def on_device(queries, positives, pages):
    count, tokens, width = queries.shape
    page = pages[0]
    patches = page.shape[0]
    query = queries.reshape(count * tokens, width)
    rows = count * tokens
    f32, bf16, i16 = jnp.float32, jnp.bfloat16, jnp.int16
    unit = 2 * rows * patches * width

    far_page = passed_along(page, "dp", 2)
    next_query = passed_along(query, "dp", -1)
    positive = jnp.repeat(positives.astype(f32), tokens)[None, :]

    unit_outs = [((patches, rows), bf16), ((width, rows), f32), ((1, rows), f32), ((1, rows), f32), ((width, rows), bf16)]
    powers_a, mixed_a, total_a, smooth_a, query_t = on_core(unit_body, unit_outs, (page, query), 2 * unit, "own_unit")
    powers_b, mixed_b, total_b, smooth_b, next_query_t = on_core(
        unit_body, unit_outs, (page, next_query), 2 * unit, "next_unit")
    powers_c, powers_d, total_far, own, onward, _ = on_core(
        functools.partial(pair_body, tokens),
        [((patches, rows), bf16), ((patches, rows), bf16), ((2, rows), f32), ((4, rows), f32), ((2, rows), f32), ((2, rows), f32)],
        (far_page, query, next_query, smooth_a, smooth_b, positive), 2 * unit, "far_units")
    from_next = passed_along(own, "dp", -1)
    from_last = passed_along(onward, "dp", 1)
    mixed_c, mixed_d = on_core(
        mix_body, [((width, rows), f32)] * 2, (far_page, powers_c, powers_d), 2 * unit, "far_mix")
    page_out, query_out, loss, weight = on_core(
        send_body,
        [((patches + PAD, width), i16), ((width + PAD, rows), i16), ((1, rows), f32), ((4, rows), f32)],
        (from_next, from_last, own, onward, total_a, total_b, total_far, query_t, next_query_t,
         powers_c, powers_d, mixed_b, mixed_d), 2 * unit, "send_terms")
    page_in = passed_along(page_out, "dp", -2)
    query_in = passed_along(query_out, "dp", 1)
    page_own, query_own = on_core(
        keep_body, [((patches, width), f32), ((width, rows), f32)],
        (weight, query_t, next_query_t, powers_a, powers_b, mixed_a, mixed_c), 2 * unit, "own_terms")
    query_grad, page_grad = pl.pallas_call(
        lambda a, b, c, d, page_ref, query_ref: last_body(a, b, c, d, page_ref, query_ref),
        out_shape=[jax.ShapeDtypeStruct((patches, width), f32), jax.ShapeDtypeStruct((rows, width), f32)],
        in_specs=[VMEM] * 4,
        out_specs=[VMEM] * 2,
        compiler_params=pltpu.CompilerParams(vmem_limit_bytes=24 * MIB),
        name="last_sum",
    )(page_own, query_own, page_in, query_in)[::-1]
    return (loss.reshape(count, tokens)[:, 0], query_grad.reshape(count, tokens, width), page_grad[None])


def solution(mesh):
    in_specs = (P("dp", None, None), P("dp"), P("dp", None, None))
    out_specs = (P("dp"), P("dp", None, None), P("dp", None, None))
    return jax.shard_map(
        on_device, mesh=mesh, in_specs=in_specs, out_specs=out_specs, check_vma=False
    )
```

```python
import functools
import math

import jax
import jax.numpy as jnp
from jax import lax
from jax.experimental import pallas as pl
from jax.experimental.pallas import tpu as pltpu
from jax.sharding import PartitionSpec as P


tau_scale = 0.1
EXPONENT = math.log2(math.e) / tau_scale
CHUNK = 256
PAD = 16
MIB = 1024 * 1024

VMEM = pl.BlockSpec(memory_space=pltpu.VMEM)
ANY = pl.BlockSpec(memory_space=pl.ANY)


def passed_along(value, axis, steps):
    count = lax.axis_size(axis)
    pairs = [(source, (source + steps) % count) for source in range(count)]
    return lax.ppermute(value, axis, pairs)


def swapped(value, axis, first):
    count = lax.axis_size(axis)
    pairs = [(source, (source + (1 if source % 2 == first else -1)) % count) for source in range(count)]
    return lax.ppermute(value, axis, pairs)


def on_core(body, outs, args, flops, name, limit=8, specs=None, scratch=()):
    return pl.pallas_call(
        body,
        out_shape=[pltpu.VMEM(shape, dtype) for shape, dtype in outs],
        in_specs=specs or [VMEM] * len(args),
        out_specs=[VMEM] * len(outs),
        scratch_shapes=list(scratch),
        compiler_params=pltpu.CompilerParams(vmem_limit_bytes=limit * MIB),
        cost_estimate=pl.CostEstimate(flops=flops, bytes_accessed=2 * MIB, transcendentals=0),
        name=name,
    )(*args)


def rows_dot(a, b):
    return lax.dot_general(a, b, (((1,), (1,)), ((), ())), preferred_element_type=jnp.float32)


def token_powers(page, query, powers_ref, total_ref, smooth_ref, row):
    rows = query.shape[0]
    for start in range(0, rows, CHUNK):
        cut = slice(start, start + CHUNK)
        products = rows_dot(page[...], query[cut, :])
        largest = jnp.max(products, axis=0, keepdims=True)
        powers = jnp.exp2((products - largest) * EXPONENT)
        total = jnp.sum(powers, axis=0, keepdims=True)
        powers_ref[:, cut] = powers.astype(jnp.bfloat16)
        total_ref[row : row + 1, cut] = total
        smooth_ref[row : row + 1, cut] = largest + tau_scale * jnp.log(total)


def mix_pages(page_t, powers_ref, mixed_ref):
    rows = powers_ref.shape[1]
    for start in range(0, rows, CHUNK):
        cut = slice(start, start + CHUNK)
        mixed_ref[:, cut] = jnp.dot(page_t, powers_ref[:, cut], preferred_element_type=jnp.float32)


def turned(value):
    return value.astype(jnp.float32).T.astype(jnp.bfloat16)


def of_token(shape, token_axis, tokens):
    token = lax.broadcasted_iota(jnp.int32, shape, token_axis)
    query = lax.broadcasted_iota(jnp.int32, shape, 1 - token_axis)
    return token, query


def own_body(tokens, page_hbm, query_hbm, positive_hbm, powers_ref, mixed_ref, total_ref, smooth_ref,
             query_t_ref, query_ref, positive_ref, page, positives, sems):
    page_copy = pltpu.make_async_copy(page_hbm, page, sems.at[0])
    query_copy = pltpu.make_async_copy(query_hbm, query_ref, sems.at[1])
    positive_copy = pltpu.make_async_copy(positive_hbm, positives, sems.at[2])
    page_copy.start()
    query_copy.start()
    positive_copy.start()
    positive_copy.wait()
    token, query = of_token((positives.shape[1], query_ref.shape[0]), 1, tokens)
    inside = (token >= query * tokens) & (token < query * tokens + tokens)
    positive_ref[...] = jnp.sum(jnp.where(inside, positives[...].astype(jnp.float32).T, 0.0), axis=0, keepdims=True)
    page_copy.wait()
    query_copy.wait()
    token_powers(page, query_ref, powers_ref, total_ref, smooth_ref, 0)
    mix_pages(turned(page[...]), powers_ref, mixed_ref)
    query_t_ref[...] = turned(query_ref[...])


def far_body(page, query, powers_ref, total_ref, smooth_ref):
    token_powers(page, query, powers_ref, total_ref, smooth_ref, 0)


def query_sums(value, tokens):
    lane = lax.broadcasted_iota(jnp.int32, value.shape, 1)
    width = value.shape[1]
    step = tokens // 2
    while step:
        ahead = pltpu.roll(value, width - step, 1)
        behind = pltpu.roll(value, step, 1)
        value = value + jnp.where((lane & step) != 0, behind, ahead)
        step //= 2
    return value


def pair_body(tokens, page, far_page, next_query, smooth_a, smooth_c, positive,
              powers_b_ref, powers_d_ref, total_ref, scores_ref, near_ref, far_ref, next_query_t_ref, smooth_ref):
    token_powers(page, next_query, powers_b_ref, total_ref, smooth_ref, 0)
    token_powers(far_page, next_query, powers_d_ref, total_ref, smooth_ref, 1)
    rows = jnp.concatenate([smooth_a[...], smooth_c[...], smooth_ref[...]], axis=0)
    sums = query_sums(rows, tokens)
    scores_ref[...] = sums
    own = jnp.concatenate([sums[0:2, :], positive[...], positive[...]], axis=0)
    onward = jnp.concatenate([sums[2:4, :], sums[2:4, :]], axis=0)
    even = lax.axis_index("dp") % 2 == 0
    near_ref[...] = jnp.where(even, onward, own)
    far_ref[0:4, :] = jnp.where(even, own, onward)
    far_ref[4:8, :] = sums
    next_query_t_ref[...] = turned(next_query[...])


def mix_body(page, far_page, powers_b, powers_c, powers_d, mixed_b_ref, mixed_c_ref, mixed_d_ref):
    mix_pages(turned(page[...]), powers_b, mixed_b_ref)
    far_page_t = turned(far_page[...])
    mix_pages(far_page_t, powers_c, mixed_c_ref)
    mix_pages(far_page_t, powers_d, mixed_d_ref)


def slopes_of(scores, positive):
    flags = [(positive == float(offset)).astype(jnp.float32) for offset in range(4)]
    positive_score = sum(flag * score for flag, score in zip(flags, scores))
    margins = [score - positive_score for score in scores]
    loss = sum((1.0 - flag) * jax.nn.softplus(margin) for flag, margin in zip(flags, margins))
    terms = [(1.0 - flag) * jax.nn.sigmoid(margin) for flag, margin in zip(flags, margins)]
    total = sum(terms)
    return loss, [term - flag * total for flag, term in zip(flags, terms)]


def to_short(value):
    largest = jnp.maximum(jnp.max(jnp.abs(value), axis=0, keepdims=True), 1e-38)
    power = jnp.minimum(jnp.floor(math.log2(32000.0) - jnp.log2(largest)), 126.0)
    short = jnp.round(value * jnp.exp2(power)).astype(jnp.int32).astype(jnp.int16)
    tail = jnp.broadcast_to(power, (PAD, value.shape[1])).astype(jnp.int32).astype(jnp.int16)
    return short, tail


def from_short(ref, rows):
    power = ref[rows : rows + PAD, :].astype(jnp.int32).astype(jnp.float32)[0:1, :]
    return ref[0:rows, :].astype(jnp.int32).astype(jnp.float32) * jnp.exp2(-power)


def scaled(query_t, weight):
    return (query_t.astype(jnp.float32) * weight).astype(jnp.bfloat16)


def send_page_body(tokens, far, near, scores, positive, total_a, total_c, total_next, query_t, next_query_t,
                   powers_a, powers_b, page_out_ref, loss_ref, weight_ref):
    even = lax.axis_index("dp") % 2 == 0
    from_last = jnp.where(even, far[0:4, :], near[...])
    from_next = jnp.where(even, near[...], far[0:4, :])
    loss, slopes = slopes_of([scores[0:1, :], from_last[0:1, :], scores[1:2, :], from_last[1:2, :]], positive[...])
    _, next_slopes = slopes_of([from_next[0:1, :], scores[2:3, :], from_next[1:2, :], scores[3:4, :]], from_next[2:3, :])
    loss_ref[...] = loss
    weight_far_a = slopes[2] / total_c[...]
    weight_far_b = next_slopes[3] / total_next[1:2, :]
    weight_ref[0:1, :] = slopes[0] / total_a[...]
    weight_ref[1:2, :] = next_slopes[1] / total_next[0:1, :]
    weight_ref[2:3, :] = weight_far_a
    weight_ref[3:4, :] = weight_far_b
    page_term = rows_dot(powers_a[...], scaled(query_t[...], weight_far_a))
    page_term = page_term + rows_dot(powers_b[...], scaled(next_query_t[...], weight_far_b))
    count = page_term.shape[0]
    short, tail = to_short(page_term)
    page_out_ref[0:count, :] = short
    page_out_ref[count : count + PAD, :] = tail
    page_out_ref[count + PAD : count + 2 * PAD, :] = tail


def send_query_body(tokens, weight, mixed_own_b, mixed_far_b, loss_all, query_out_ref, loss_ref):
    query_term = (mixed_own_b[...] * weight[1:2, :] + mixed_far_b[...] * weight[3:4, :]).T
    count = query_term.shape[0]
    short, tail = to_short(query_term)
    query_out_ref[0:count, :] = short
    query_out_ref[count : count + PAD, :] = tail
    token, query = of_token((loss_ref.shape[1], loss_all.shape[1]), 1, tokens)
    loss_ref[...] = jnp.sum(jnp.where(token == query * tokens, loss_all[...], 0.0), axis=1, keepdims=True).T


def keep_body(weight, query_t, next_query_t, powers_a, powers_b, mixed_own_a, mixed_far_a,
              page_ref, query_ref):
    page_term = rows_dot(powers_a[...], scaled(query_t[...], weight[0:1, :]))
    page_ref[...] = page_term + rows_dot(powers_b[...], scaled(next_query_t[...], weight[1:2, :]))
    query_ref[...] = (mixed_own_a[...] * weight[0:1, :] + mixed_far_a[...] * weight[2:3, :]).T


def sum_body(own, arrived, sum_ref):
    sum_ref[...] = own[...] + from_short(arrived, own.shape[0])


def finish(body, shape, args, name):
    return pl.pallas_call(
        body,
        out_shape=jax.ShapeDtypeStruct(shape, jnp.float32),
        in_specs=[VMEM] * len(args),
        out_specs=VMEM,
        compiler_params=pltpu.CompilerParams(vmem_limit_bytes=4 * MIB),
        cost_estimate=pl.CostEstimate(flops=1000, bytes_accessed=1000, transcendentals=0),
        name=name,
    )(*args)


def in_hbm(value):
    return pltpu.with_memory_space_constraint(value, pltpu.HBM)


def on_device(queries, positives, pages):
    count, tokens, width = queries.shape
    page = pages[0]
    patches = page.shape[0]
    query = queries.reshape(count * tokens, width)
    rows = count * tokens
    f32, bf16, i16 = jnp.float32, jnp.bfloat16, jnp.int16
    unit = 2 * rows * patches * width

    far_page = passed_along(page, "dp", 2)
    next_query = passed_along(query, "dp", -1)

    powers_a, mixed_a, total_a, smooth_a, query_t, own_query, positive, own_page = on_core(
        functools.partial(own_body, tokens),
        [((patches, rows), bf16), ((width, rows), f32), ((1, rows), f32), ((1, rows), f32), ((width, rows), bf16),
         ((rows, width), bf16), ((1, rows), f32), ((patches, width), bf16)],
        tuple(in_hbm(value) for value in (page, query, positives[None])), 2 * unit, "own_unit", specs=[ANY] * 3,
        scratch=[pltpu.VMEM((1, count), jnp.int32), pltpu.SemaphoreType.DMA((3,))])
    powers_c, total_c, smooth_c = on_core(
        far_body, [((patches, rows), bf16), ((1, rows), f32), ((1, rows), f32)], (far_page, own_query), unit, "far_unit")
    powers_b, powers_d, total_next, scores, near, far, next_query_t = on_core(
        functools.partial(pair_body, tokens),
        [((patches, rows), bf16), ((patches, rows), bf16), ((2, rows), f32), ((4, rows), f32), ((4, rows), f32), ((8, rows), f32),
         ((width, rows), bf16)],
        (own_page, far_page, next_query, smooth_a, smooth_c, positive), 2 * unit, "next_units",
        scratch=[pltpu.VMEM((2, rows), f32)])
    far = swapped(far, "dp", 1)
    near = swapped(near, "dp", 0)
    mixed_b, mixed_c, mixed_d = on_core(
        mix_body, [((width, rows), f32)] * 3, (own_page, far_page, powers_b, powers_c, powers_d), 3 * unit, "mixes")
    page_out, loss_all, weight = on_core(
        functools.partial(send_page_body, tokens),
        [((patches + 2 * PAD, width), i16), ((1, rows), f32), ((4, rows), f32)],
        (far, near, scores, positive, total_a, total_c, total_next, query_t, next_query_t,
         powers_c, powers_d), 2 * unit, "send_page")
    page_in = passed_along(page_out, "dp", -2)
    query_out, loss = on_core(
        functools.partial(send_query_body, tokens),
        [((rows + PAD, width), i16), ((1, count), f32)],
        (weight, mixed_b, mixed_d, loss_all), unit, "send_query")
    query_in = passed_along(query_out, "dp", 1)
    page_own, query_own = on_core(
        keep_body, [((patches, width), f32), ((rows, width), f32)],
        (weight, query_t, next_query_t, powers_a, powers_b, mixed_a, mixed_c), 2 * unit, "own_terms")
    query_grad = finish(sum_body, (rows, width), (query_own, query_in), "query_sum")
    page_own, query_grad = lax.optimization_barrier((page_own, query_grad))
    page_grad = finish(sum_body, (patches, width), (page_own, page_in), "page_sum")
    return (loss[0], query_grad.reshape(count, tokens, width), page_grad[None])


def solution(mesh):
    in_specs = (P("dp", None, None), P("dp"), P("dp", None, None))
    out_specs = (P("dp"), P("dp", None, None), P("dp", None, None))
    return jax.shard_map(
        on_device, mesh=mesh, in_specs=in_specs, out_specs=out_specs, check_vma=False
    )
```

```python
import functools
import math

import jax
import jax.numpy as jnp
from jax import lax
from jax.experimental import pallas as pl
from jax.experimental.pallas import tpu as pltpu
from jax.sharding import PartitionSpec as P


tau_scale = 0.1
EXPONENT = math.log2(math.e) / tau_scale
CHUNK = 256
PAD = 16
MIB = 1024 * 1024

VMEM = pl.BlockSpec(memory_space=pltpu.VMEM)
ANY = pl.BlockSpec(memory_space=pl.ANY)


def passed_along(value, axis, steps):
    count = lax.axis_size(axis)
    pairs = [(source, (source + steps) % count) for source in range(count)]
    return lax.ppermute(value, axis, pairs)


def odd_passed_along(value, axis, steps):
    count = lax.axis_size(axis)
    pairs = [(source, (source + steps) % count if source % 2 else source) for source in range(count)]
    return lax.ppermute(value, axis, pairs)


def swapped(value, axis):
    return lax.ppermute(value, axis, [(source, source ^ 1) for source in range(lax.axis_size(axis))])


def on_core(body, outs, args, flops, name, limit=8, specs=None, scratch=()):
    return pl.pallas_call(
        body,
        out_shape=[pltpu.VMEM(shape, dtype) for shape, dtype in outs],
        in_specs=specs or [VMEM] * len(args),
        out_specs=[VMEM] * len(outs),
        scratch_shapes=list(scratch),
        compiler_params=pltpu.CompilerParams(vmem_limit_bytes=limit * MIB),
        cost_estimate=pl.CostEstimate(flops=flops, bytes_accessed=2 * MIB, transcendentals=0),
        name=name,
    )(*args)


def rows_dot(a, b):
    return lax.dot_general(a, b, (((1,), (1,)), ((), ())), preferred_element_type=jnp.float32)


def token_powers(page, query, powers_ref, total_ref, smooth_ref, row):
    rows = query.shape[0]
    for start in range(0, rows, CHUNK):
        cut = slice(start, start + CHUNK)
        products = rows_dot(page[...], query[cut, :])
        largest = jnp.max(products, axis=0, keepdims=True)
        powers = jnp.exp2((products - largest) * EXPONENT)
        total = jnp.sum(powers, axis=0, keepdims=True)
        powers_ref[:, cut] = powers.astype(jnp.bfloat16)
        total_ref[row : row + 1, cut] = total
        smooth_ref[row : row + 1, cut] = largest + tau_scale * jnp.log(total)


def mix_pages(page_t, powers_ref, mixed_ref):
    rows = powers_ref.shape[1]
    for start in range(0, rows, CHUNK):
        cut = slice(start, start + CHUNK)
        mixed_ref[:, cut] = jnp.dot(page_t, powers_ref[:, cut], preferred_element_type=jnp.float32)


def turned(value):
    return value.astype(jnp.float32).T.astype(jnp.bfloat16)


def of_token(shape, token_axis, tokens):
    token = lax.broadcasted_iota(jnp.int32, shape, token_axis)
    query = lax.broadcasted_iota(jnp.int32, shape, 1 - token_axis)
    return token, query


def own_body(tokens, page_hbm, query_hbm, positive_hbm, powers_ref, mixed_ref, total_ref, smooth_ref,
             query_t_ref, query_ref, positive_ref, page, positives, sems):
    page_copy = pltpu.make_async_copy(page_hbm, page, sems.at[0])
    query_copy = pltpu.make_async_copy(query_hbm, query_ref, sems.at[1])
    positive_copy = pltpu.make_async_copy(positive_hbm, positives, sems.at[2])
    page_copy.start()
    query_copy.start()
    positive_copy.start()
    positive_copy.wait()
    token, query = of_token((positives.shape[1], query_ref.shape[0]), 1, tokens)
    inside = (token >= query * tokens) & (token < query * tokens + tokens)
    positive_ref[...] = jnp.sum(jnp.where(inside, positives[...].astype(jnp.float32).T, 0.0), axis=0, keepdims=True)
    page_copy.wait()
    query_copy.wait()
    token_powers(page, query_ref, powers_ref, total_ref, smooth_ref, 0)
    mix_pages(turned(page[...]), powers_ref, mixed_ref)
    query_t_ref[...] = turned(query_ref[...])


def far_body(page, query, powers_ref, total_ref, smooth_ref):
    token_powers(page, query, powers_ref, total_ref, smooth_ref, 0)


def query_sums(value, tokens):
    lane = lax.broadcasted_iota(jnp.int32, value.shape, 1)
    width = value.shape[1]
    step = tokens // 2
    while step:
        ahead = pltpu.roll(value, width - step, 1)
        behind = pltpu.roll(value, step, 1)
        value = value + jnp.where((lane & step) != 0, behind, ahead)
        step //= 2
    return value


def mate_body(tokens, far_page, last_page, mate_query, smooth_a, smooth_c, positive,
              powers_d_ref, powers_b_ref, total_ref, message_ref, smooth_ref):
    token_powers(far_page, mate_query, powers_d_ref, total_ref, smooth_ref, 0)
    token_powers(last_page, mate_query, powers_b_ref, total_ref, smooth_ref, 1)
    sums = query_sums(jnp.concatenate([smooth_a[...], smooth_c[...], smooth_ref[...]], axis=0), tokens)
    message_ref[0:4, :] = sums
    message_ref[4:5, :] = positive[...]
    message_ref[5:8, :] = sums[0:3, :]


def mix_body(last_page, far_page, mate_query, powers_b, powers_c, powers_d,
             mixed_b_ref, mixed_c_ref, mixed_d_ref, mate_query_t_ref):
    mate_query_t_ref[...] = turned(mate_query[...])
    mix_pages(turned(last_page[...]), powers_b, mixed_b_ref)
    far_page_t = turned(far_page[...])
    mix_pages(far_page_t, powers_c, mixed_c_ref)
    mix_pages(far_page_t, powers_d, mixed_d_ref)


def slopes_of(scores, positive):
    flags = [(positive == float(offset)).astype(jnp.float32) for offset in range(4)]
    positive_score = sum(flag * score for flag, score in zip(flags, scores))
    margins = [score - positive_score for score in scores]
    loss = sum((1.0 - flag) * jax.nn.softplus(margin) for flag, margin in zip(flags, margins))
    terms = [(1.0 - flag) * jax.nn.sigmoid(margin) for flag, margin in zip(flags, margins)]
    total = sum(terms)
    return loss, [term - flag * total for flag, term in zip(flags, terms)]


def to_short(value):
    largest = jnp.maximum(jnp.max(jnp.abs(value), axis=0, keepdims=True), 1e-38)
    power = jnp.minimum(jnp.floor(math.log2(32000.0) - jnp.log2(largest)), 126.0)
    short = jnp.round(value * jnp.exp2(power)).astype(jnp.int32).astype(jnp.int16)
    tail = jnp.broadcast_to(power, (PAD, value.shape[1])).astype(jnp.int32).astype(jnp.int16)
    return short, tail


def from_short(ref, rows):
    power = ref[rows : rows + PAD, :].astype(jnp.int32).astype(jnp.float32)[0:1, :]
    return ref[0:rows, :].astype(jnp.int32).astype(jnp.float32) * jnp.exp2(-power)


def scaled(query_t, weight):
    return (query_t.astype(jnp.float32) * weight).astype(jnp.bfloat16)


def put_short(ref, value):
    count = value.shape[0]
    short, tail = to_short(value)
    ref[0:count, :] = short
    for start in range(count, ref.shape[0], PAD):
        ref[start : start + PAD, :] = tail


def send_last_body(message, arrived, total_a, total_c, total_mate, mate_query_t, powers_b,
                   out_ref, loss_ref, weight_ref):
    even = lax.axis_index("dp") % 2 == 0
    own = message[...]
    mate = arrived[...]
    loss, slopes = slopes_of(
        [own[0:1], jnp.where(even, mate[2:3], mate[3:4]), own[1:2], jnp.where(even, mate[3:4], mate[2:3])], own[4:5])
    _, mate_slopes = slopes_of(
        [mate[0:1], jnp.where(even, own[3:4], own[2:3]), mate[1:2], jnp.where(even, own[2:3], own[3:4])], mate[4:5])
    loss_ref[...] = loss
    weight_b = jnp.where(even, mate_slopes[1], mate_slopes[3]) / total_mate[1:2, :]
    weight_ref[0:1, :] = slopes[0] / total_a[...]
    weight_ref[1:2, :] = weight_b
    weight_ref[2:3, :] = slopes[2] / total_c[...]
    weight_ref[3:4, :] = jnp.where(even, mate_slopes[3], mate_slopes[1]) / total_mate[0:1, :]
    put_short(out_ref, rows_dot(powers_b[...], scaled(mate_query_t[...], weight_b)))


def send_far_body(weight, query_t, mate_query_t, powers_c, powers_d, out_ref):
    page_term = rows_dot(powers_c[...], scaled(query_t[...], weight[2:3, :]))
    put_short(out_ref, page_term + rows_dot(powers_d[...], scaled(mate_query_t[...], weight[3:4, :])))


def send_query_body(tokens, weight, mixed_b, mixed_d, loss_all, out_ref, loss_ref):
    put_short(out_ref, (mixed_b[...] * weight[1:2, :] + mixed_d[...] * weight[3:4, :]).T)
    token, query = of_token((loss_ref.shape[1], loss_all.shape[1]), 1, tokens)
    loss_ref[...] = jnp.sum(jnp.where(token == query * tokens, loss_all[...], 0.0), axis=1, keepdims=True).T


def keep_body(weight, query_t, powers_a, mixed_a, mixed_c, page_ref, query_ref):
    page_ref[...] = rows_dot(powers_a[...], scaled(query_t[...], weight[0:1, :]))
    query_ref[...] = (mixed_a[...] * weight[0:1, :] + mixed_c[...] * weight[2:3, :]).T


def sum_body(own, *refs):
    total = own[...]
    for arrived in refs[:-1]:
        total = total + from_short(arrived, own.shape[0])
    refs[-1][...] = total


def finish(body, shape, args, name):
    return pl.pallas_call(
        body,
        out_shape=jax.ShapeDtypeStruct(shape, jnp.float32),
        in_specs=[VMEM] * len(args),
        out_specs=VMEM,
        compiler_params=pltpu.CompilerParams(vmem_limit_bytes=4 * MIB),
        cost_estimate=pl.CostEstimate(flops=1000, bytes_accessed=1000, transcendentals=0),
        name=name,
    )(*args)


def in_hbm(value):
    return pltpu.with_memory_space_constraint(value, pltpu.HBM)


def on_device(queries, positives, pages):
    count, tokens, width = queries.shape
    page = pages[0]
    patches = page.shape[0]
    query = queries.reshape(count * tokens, width)
    rows = count * tokens
    f32, bf16, i16 = jnp.float32, jnp.bfloat16, jnp.int16
    unit = 2 * rows * patches * width

    far_page = passed_along(page, "dp", 2)
    last_page = odd_passed_along(page, "dp", 4)
    mate_query = swapped(query, "dp")

    powers_a, mixed_a, total_a, smooth_a, query_t, own_query, positive = on_core(
        functools.partial(own_body, tokens),
        [((patches, rows), bf16), ((width, rows), f32), ((1, rows), f32), ((1, rows), f32), ((width, rows), bf16),
         ((rows, width), bf16), ((1, rows), f32)],
        tuple(in_hbm(value) for value in (page, query, positives[None])), 2 * unit, "own_unit", specs=[ANY] * 3,
        scratch=[pltpu.VMEM((patches, width), bf16), pltpu.VMEM((1, count), jnp.int32), pltpu.SemaphoreType.DMA((3,))])
    powers_c, total_c, smooth_c = on_core(
        far_body, [((patches, rows), bf16), ((1, rows), f32), ((1, rows), f32)], (far_page, own_query), unit, "far_unit")
    powers_d, powers_b, total_mate, message = on_core(
        functools.partial(mate_body, tokens),
        [((patches, rows), bf16), ((patches, rows), bf16), ((2, rows), f32), ((8, rows), f32)],
        (far_page, last_page, mate_query, smooth_a, smooth_c, positive), 2 * unit, "mate_units",
        scratch=[pltpu.VMEM((2, rows), f32)])
    arrived = swapped(message, "dp")
    mixed_b, mixed_c, mixed_d, mate_query_t = on_core(
        mix_body, [((width, rows), f32)] * 3 + [((width, rows), bf16)],
        (last_page, far_page, mate_query, powers_b, powers_c, powers_d), 3 * unit, "mixes")
    last_out, loss_all, weight = on_core(
        send_last_body,
        [((patches + 4 * PAD, width), i16), ((1, rows), f32), ((4, rows), f32)],
        (message, arrived, total_a, total_c, total_mate, mate_query_t, powers_b), unit, "send_last")
    last_in = odd_passed_along(last_out, "dp", -4)
    far_out, = on_core(
        send_far_body, [((patches + 3 * PAD, width), i16)],
        (weight, query_t, mate_query_t, powers_c, powers_d), 2 * unit, "send_far")
    far_in = passed_along(far_out, "dp", -2)
    query_out, loss = on_core(
        functools.partial(send_query_body, tokens),
        [((rows + PAD, width), i16), ((1, count), f32)],
        (weight, mixed_b, mixed_d, loss_all), 1000, "send_query")
    query_in = swapped(query_out, "dp")
    page_own, query_own = on_core(
        keep_body, [((patches, width), f32), ((rows, width), f32)],
        (weight, query_t, powers_a, mixed_a, mixed_c), 1000, "own_terms")
    query_grad = finish(sum_body, (rows, width), (query_own, query_in), "query_sum")
    page_own, query_grad = lax.optimization_barrier((page_own, query_grad))
    page_grad = finish(sum_body, (patches, width), (page_own, far_in, last_in), "page_sum")
    return (loss[0], query_grad.reshape(count, tokens, width), page_grad[None])


def solution(mesh):
    in_specs = (P("dp", None, None), P("dp"), P("dp", None, None))
    out_specs = (P("dp"), P("dp", None, None), P("dp", None, None))
    return jax.shard_map(
        on_device, mesh=mesh, in_specs=in_specs, out_specs=out_specs, check_vma=False
    )
```

```python
import functools
import math

import jax
import jax.numpy as jnp
from jax import lax
from jax.experimental import pallas as pl
from jax.experimental.pallas import tpu as pltpu
from jax.sharding import PartitionSpec as P


tau_scale = 0.1
EXPONENT = math.log2(math.e) / tau_scale
CHUNK = 128
COLUMNS = 8
PAD = 16
MIB = 1024 * 1024

VMEM = pl.BlockSpec(memory_space=pltpu.VMEM)
ANY = pl.BlockSpec(memory_space=pl.ANY)


def passed_along(value, axis, steps):
    count = lax.axis_size(axis)
    pairs = [(source, (source + steps) % count) for source in range(count)]
    return lax.ppermute(value, axis, pairs)


def odd_passed_along(value, axis, steps):
    count = lax.axis_size(axis)
    pairs = [(source, (source + steps) % count if source % 2 else source) for source in range(count)]
    return lax.ppermute(value, axis, pairs)


def swapped(value, axis):
    return lax.ppermute(value, axis, [(source, source ^ 1) for source in range(lax.axis_size(axis))])


def on_core(body, outs, args, flops, name, limit=8, specs=None, scratch=()):
    return pl.pallas_call(
        body,
        out_shape=[pltpu.VMEM(shape, dtype) for shape, dtype in outs],
        in_specs=specs or [VMEM] * len(args),
        out_specs=[VMEM] * len(outs),
        scratch_shapes=list(scratch),
        compiler_params=pltpu.CompilerParams(vmem_limit_bytes=limit * MIB),
        cost_estimate=pl.CostEstimate(flops=flops, bytes_accessed=2 * MIB, transcendentals=0),
        name=name,
    )(*args)


def rows_dot(a, b):
    return lax.dot_general(a, b, (((1,), (1,)), ((), ())), preferred_element_type=jnp.float32)


def token_powers(page, query, powers_ref, stats_ref, unit):
    rows = query.shape[0]
    for start in range(0, rows, CHUNK):
        cut = slice(start, start + CHUNK)
        products = rows_dot(query[cut, :], page[...])
        largest = jnp.max(products, axis=1, keepdims=True)
        powers = jnp.exp2((products - largest) * EXPONENT)
        powers_ref[cut, :] = powers.astype(jnp.bfloat16)
        stats_ref[cut, 2 * unit : 2 * unit + 1] = largest
        stats_ref[cut, 2 * unit + 1 : 2 * unit + 2] = jnp.sum(powers, axis=1, keepdims=True)


def token_rows(stats_ref, units, total_ref):
    stats = stats_ref[...].T
    smooth = []
    for unit in range(units):
        total = stats[2 * unit + 1 : 2 * unit + 2, :]
        total_ref[unit : unit + 1, :] = total
        smooth.append(stats[2 * unit : 2 * unit + 1, :] + tau_scale * jnp.log(total))
    return smooth


def mix_pages(page, powers_ref, mixed_ref):
    mixed_ref[...] = jnp.dot(powers_ref[...], page[...], preferred_element_type=jnp.float32)


def page_terms(query_t, weight, powers_ref):
    return jnp.dot(scaled(query_t[...], weight), powers_ref[...], preferred_element_type=jnp.float32)


def weight_columns(weight):
    return jnp.concatenate([weight[...], weight[...]], axis=0).T


def turned(value):
    return value.astype(jnp.float32).T.astype(jnp.bfloat16)


def of_token(shape, token_axis, tokens):
    token = lax.broadcasted_iota(jnp.int32, shape, token_axis)
    query = lax.broadcasted_iota(jnp.int32, shape, 1 - token_axis)
    return token, query


def own_body(tokens, page_hbm, query_hbm, positive_hbm, powers_ref, mixed_ref, total_ref, smooth_ref,
             query_t_ref, query_ref, positive_ref, page, positives, sems, stats):
    page_copy = pltpu.make_async_copy(page_hbm, page, sems.at[0])
    query_copy = pltpu.make_async_copy(query_hbm, query_ref, sems.at[1])
    positive_copy = pltpu.make_async_copy(positive_hbm, positives, sems.at[2])
    page_copy.start()
    query_copy.start()
    positive_copy.start()
    positive_copy.wait()
    token, query = of_token((positives.shape[1], query_ref.shape[0]), 1, tokens)
    inside = (token >= query * tokens) & (token < query * tokens + tokens)
    positive_ref[...] = jnp.sum(jnp.where(inside, positives[...].astype(jnp.float32).T, 0.0), axis=0, keepdims=True)
    page_copy.wait()
    query_copy.wait()
    token_powers(page, query_ref, powers_ref, stats, 0)
    smooth_ref[...] = token_rows(stats, 1, total_ref)[0]
    mix_pages(page, powers_ref, mixed_ref)
    query_t_ref[...] = turned(query_ref[...])


def far_body(page, query, powers_ref, total_ref, smooth_ref, stats):
    token_powers(page, query, powers_ref, stats, 0)
    smooth_ref[...] = token_rows(stats, 1, total_ref)[0]


def query_sums(value, tokens):
    lane = lax.broadcasted_iota(jnp.int32, value.shape, 1)
    width = value.shape[1]
    step = tokens // 2
    while step:
        ahead = pltpu.roll(value, width - step, 1)
        behind = pltpu.roll(value, step, 1)
        value = value + jnp.where((lane & step) != 0, behind, ahead)
        step //= 2
    return value


def mate_body(page, query, smooth_c, powers_ref, total_ref, smooth_ref, stats):
    token_powers(page, query, powers_ref, stats, 0)
    smooth_ref[0:1, :] = smooth_c[...]
    smooth_ref[1:2, :] = token_rows(stats, 1, total_ref)[0]


def last_body(tokens, page, mate_query, smooth_a, smooth_far, positive,
              powers_ref, total_ref, message_ref, stats):
    token_powers(page, mate_query, powers_ref, stats, 0)
    smooth = token_rows(stats, 1, total_ref)
    sums = query_sums(jnp.concatenate([smooth_a[...], smooth_far[...]] + smooth, axis=0), tokens)
    message_ref[0:4, :] = sums
    message_ref[4:5, :] = positive[...]
    message_ref[5:8, :] = sums[0:3, :]


def mix_body(far_page, mate_query, powers_c, powers_d, mixed_c_ref, mixed_d_ref, mate_query_t_ref):
    mate_query_t_ref[...] = turned(mate_query[...])
    mix_pages(far_page, powers_c, mixed_c_ref)
    mix_pages(far_page, powers_d, mixed_d_ref)


def slopes_of(scores, positive):
    flags = [(positive == float(offset)).astype(jnp.float32) for offset in range(4)]
    positive_score = sum(flag * score for flag, score in zip(flags, scores))
    margins = [score - positive_score for score in scores]
    loss = sum((1.0 - flag) * jax.nn.softplus(margin) for flag, margin in zip(flags, margins))
    terms = [(1.0 - flag) * jax.nn.sigmoid(margin) for flag, margin in zip(flags, margins)]
    total = sum(terms)
    return loss, [term - flag * total for flag, term in zip(flags, terms)]


def to_short(value):
    largest = jnp.maximum(jnp.max(jnp.abs(value), axis=0, keepdims=True), 1e-38)
    power = jnp.minimum(jnp.floor(math.log2(32000.0) - jnp.log2(largest)), 126.0)
    short = jnp.round(value * jnp.exp2(power)).astype(jnp.int32).astype(jnp.int16)
    tail = jnp.broadcast_to(power, (PAD, value.shape[1])).astype(jnp.int32).astype(jnp.int16)
    return short, tail


def from_short(ref, rows):
    power = ref[rows : rows + PAD, :].astype(jnp.int32).astype(jnp.float32)[0:1, :]
    return ref[0:rows, :].astype(jnp.int32).astype(jnp.float32) * jnp.exp2(-power)


def scaled(query_t, weight):
    return (query_t.astype(jnp.float32) * weight).astype(jnp.bfloat16)


def put_short(ref, value):
    count = value.shape[0]
    short, tail = to_short(value)
    ref[0:count, :] = short
    for start in range(count, ref.shape[0], PAD):
        ref[start : start + PAD, :] = tail


def send_last_body(message, arrived, total_a, total_c, total_d, total_b, mate_query_t, powers_b,
                   out_ref, loss_ref, weight_ref):
    even = lax.axis_index("dp") % 2 == 0
    own = message[...]
    mate = arrived[...]
    loss, slopes = slopes_of(
        [own[0:1], jnp.where(even, mate[2:3], mate[3:4]), own[1:2], jnp.where(even, mate[3:4], mate[2:3])], own[4:5])
    _, mate_slopes = slopes_of(
        [mate[0:1], jnp.where(even, own[3:4], own[2:3]), mate[1:2], jnp.where(even, own[2:3], own[3:4])], mate[4:5])
    loss_ref[...] = loss
    weight_b = jnp.where(even, mate_slopes[1], mate_slopes[3]) / total_b[...]
    weight_ref[0:1, :] = slopes[0] / total_a[...]
    weight_ref[1:2, :] = weight_b
    weight_ref[2:3, :] = slopes[2] / total_c[...]
    weight_ref[3:4, :] = jnp.where(even, mate_slopes[3], mate_slopes[1]) / total_d[...]
    put_short(out_ref, page_terms(mate_query_t, weight_b, powers_b).T)


def send_far_body(weight, query_t, mate_query_t, powers_c, powers_d, out_ref):
    term = page_terms(query_t, weight[2:3, :], powers_c) + page_terms(mate_query_t, weight[3:4, :], powers_d)
    put_short(out_ref, term.T)


def send_query_body(tokens, weight, last_page, powers_b, mixed_d, loss_all, out_ref, loss_ref):
    mixed_b = jnp.dot(powers_b[...], last_page[...], preferred_element_type=jnp.float32)
    columns = weight_columns(weight)
    put_short(out_ref, mixed_b * columns[:, 1:2] + mixed_d[...] * columns[:, 3:4])
    token, query = of_token((loss_ref.shape[1], loss_all.shape[1]), 1, tokens)
    loss_ref[...] = jnp.sum(jnp.where(token == query * tokens, loss_all[...], 0.0), axis=1, keepdims=True).T


def keep_body(weight, query_t, powers_a, mixed_a, mixed_c, page_ref, query_ref):
    columns = weight_columns(weight)
    page_ref[...] = page_terms(query_t, weight[0:1, :], powers_a).T
    query_ref[...] = mixed_a[...] * columns[:, 0:1] + mixed_c[...] * columns[:, 2:3]


def sum_body(own, *refs):
    total = own[...]
    for arrived in refs[:-1]:
        total = total + from_short(arrived, own.shape[0])
    refs[-1][...] = total


def last_sums_body(query_own, query_in, loss_row, page_own, far_in, last_in, query_ref, loss_ref, page_ref):
    sum_body(query_own, query_in, query_ref)
    loss_ref[...] = loss_row[0, :]
    sum_body(page_own, far_in, last_in, page_ref)


def last_sums(query_own, query_in, loss_row, page_own, far_in, last_in):
    shapes = (query_own.shape, loss_row.shape[1:], page_own.shape)
    return pl.pallas_call(
        last_sums_body,
        out_shape=[jax.ShapeDtypeStruct(shape, jnp.float32) for shape in shapes],
        in_specs=[VMEM] * 6,
        out_specs=[VMEM] * 3,
        compiler_params=pltpu.CompilerParams(vmem_limit_bytes=4 * MIB),
        cost_estimate=pl.CostEstimate(flops=1000, bytes_accessed=1000, transcendentals=0),
        name="last_sums",
    )(query_own, query_in, loss_row, page_own, far_in, last_in)


def in_hbm(value):
    return pltpu.with_memory_space_constraint(value, pltpu.HBM)


def on_device(queries, positives, pages):
    count, tokens, width = queries.shape
    page = pages[0]
    patches = page.shape[0]
    query = queries.reshape(count * tokens, width)
    rows = count * tokens
    f32, bf16, i16 = jnp.float32, jnp.bfloat16, jnp.int16
    unit = 2 * rows * patches * width

    far_page = passed_along(page, "dp", 2)
    last_page = odd_passed_along(page, "dp", 4)
    mate_query = swapped(query, "dp")

    powers_a, mixed_a, total_a, smooth_a, query_t, own_query, positive = on_core(
        functools.partial(own_body, tokens),
        [((rows, patches), bf16), ((rows, width), f32), ((1, rows), f32), ((1, rows), f32), ((width, rows), bf16),
         ((rows, width), bf16), ((1, rows), f32)],
        tuple(in_hbm(value) for value in (page, query, positives[None])), 2 * unit, "own_unit", specs=[ANY] * 3,
        scratch=[pltpu.VMEM((patches, width), bf16), pltpu.VMEM((1, count), jnp.int32), pltpu.SemaphoreType.DMA((3,)),
                 pltpu.VMEM((rows, COLUMNS), f32)])
    powers_c, total_c, smooth_c = on_core(
        far_body, [((rows, patches), bf16), ((1, rows), f32), ((1, rows), f32)], (far_page, own_query), unit, "far_unit",
        scratch=[pltpu.VMEM((rows, COLUMNS), f32)])
    powers_d, total_d, smooth_far = on_core(
        mate_body, [((rows, patches), bf16), ((1, rows), f32), ((2, rows), f32)],
        (far_page, mate_query, smooth_c), unit, "mate_unit",
        scratch=[pltpu.VMEM((rows, COLUMNS), f32)])
    powers_b, total_b, message = on_core(
        functools.partial(last_body, tokens),
        [((rows, patches), bf16), ((1, rows), f32), ((8, rows), f32)],
        (last_page, mate_query, smooth_a, smooth_far, positive), unit, "last_unit",
        scratch=[pltpu.VMEM((rows, COLUMNS), f32)])
    arrived = swapped(message, "dp")
    mixed_c, mixed_d, mate_query_t = on_core(
        mix_body, [((rows, width), f32)] * 2 + [((width, rows), bf16)],
        (far_page, mate_query, powers_c, powers_d), 2 * unit, "mixes")
    last_out, loss_all, weight = on_core(
        send_last_body,
        [((patches + 4 * PAD, width), i16), ((1, rows), f32), ((4, rows), f32)],
        (message, arrived, total_a, total_c, total_d, total_b, mate_query_t, powers_b), unit, "send_last")
    last_in = odd_passed_along(last_out, "dp", -4)
    far_out, = on_core(
        send_far_body, [((patches + 3 * PAD, width), i16)],
        (weight, query_t, mate_query_t, powers_c, powers_d), 2 * unit, "send_far")
    far_in = passed_along(far_out, "dp", -2)
    query_out, loss = on_core(
        functools.partial(send_query_body, tokens),
        [((rows + PAD, width), i16), ((1, count), f32)],
        (weight, last_page, powers_b, mixed_d, loss_all), 1000, "send_query")
    query_in = swapped(query_out, "dp")
    page_own, query_own = on_core(
        keep_body, [((patches, width), f32), ((rows, width), f32)],
        (weight, query_t, powers_a, mixed_a, mixed_c), 1000, "own_terms")
    query_grad, loss, page_grad = last_sums(query_own, query_in, loss, page_own, far_in, last_in)
    return (loss, query_grad.reshape(count, tokens, width), page_grad[None])


def solution(mesh):
    in_specs = (P("dp", None, None), P("dp"), P("dp", None, None))
    out_specs = (P("dp"), P("dp", None, None), P("dp", None, None))
    return jax.shard_map(
        on_device, mesh=mesh, in_specs=in_specs, out_specs=out_specs, check_vma=False
    )
```

```python
import functools
import math

import jax
import jax.numpy as jnp
from jax import lax
from jax.experimental import pallas as pl
from jax.experimental.pallas import tpu as pltpu
from jax.sharding import PartitionSpec as P


tau_scale = 0.1
EXPONENT = math.log2(math.e) / tau_scale
CHUNK = 128
COLUMNS = 8
LANES = 128
PAD = 16
MIB = 1024 * 1024

VMEM = pl.BlockSpec(memory_space=pltpu.VMEM)
ANY = pl.BlockSpec(memory_space=pl.ANY)


def passed_along(value, axis, steps):
    count = lax.axis_size(axis)
    pairs = [(source, (source + steps) % count) for source in range(count)]
    return lax.ppermute(value, axis, pairs)


def odd_passed_along(value, axis, steps):
    count = lax.axis_size(axis)
    pairs = [(source, (source + steps) % count if source % 2 else source) for source in range(count)]
    return lax.ppermute(value, axis, pairs)


def swapped(value, axis):
    return lax.ppermute(value, axis, [(source, source ^ 1) for source in range(lax.axis_size(axis))])


def on_core(body, outs, args, flops, name, limit=8, specs=None, scratch=()):
    return pl.pallas_call(
        body,
        out_shape=[pltpu.VMEM(shape, dtype) for shape, dtype in outs],
        in_specs=specs or [VMEM] * len(args),
        out_specs=[VMEM] * len(outs),
        scratch_shapes=list(scratch),
        compiler_params=pltpu.CompilerParams(vmem_limit_bytes=limit * MIB),
        cost_estimate=pl.CostEstimate(flops=flops, bytes_accessed=2 * MIB, transcendentals=0),
        name=name,
    )(*args)


def rows_dot(a, b):
    return lax.dot_general(a, b, (((1,), (1,)), ((), ())), preferred_element_type=jnp.float32)


def token_powers(page, query, powers_ref, stats_ref, unit):
    rows = query.shape[0]
    for start in range(0, rows, CHUNK):
        cut = slice(start, start + CHUNK)
        products = rows_dot(query[cut, :], page[...])
        largest = jnp.max(products, axis=1, keepdims=True)
        powers = jnp.exp2((products - largest) * EXPONENT)
        powers_ref[cut, :] = powers.astype(jnp.bfloat16)
        stats_ref[cut, 2 * unit : 2 * unit + 1] = largest
        stats_ref[cut, 2 * unit + 1 : 2 * unit + 2] = jnp.sum(powers, axis=1, keepdims=True)


def token_rows(stats_ref, units, total_ref):
    stats = stats_ref[...].T
    smooth = []
    for unit in range(units):
        total = stats[2 * unit + 1 : 2 * unit + 2, :]
        total_ref[unit : unit + 1, :] = total
        smooth.append(stats[2 * unit : 2 * unit + 1, :] + tau_scale * jnp.log(total))
    return smooth


def mix_pages(page, powers_ref, mixed_ref):
    mixed_ref[...] = jnp.dot(powers_ref[...], page[...], preferred_element_type=jnp.float32)


def page_terms(query_t, weight, powers_ref):
    return jnp.dot(scaled(query_t[...], weight), powers_ref[...], preferred_element_type=jnp.float32)


def weight_columns(weight):
    return jnp.concatenate([weight[...], weight[...]], axis=0).T


def turned(value):
    return value.astype(jnp.float32).T.astype(jnp.bfloat16)


def of_token(shape, token_axis, tokens):
    token = lax.broadcasted_iota(jnp.int32, shape, token_axis)
    query = lax.broadcasted_iota(jnp.int32, shape, 1 - token_axis)
    return token, query


def own_body(tokens, page_hbm, query_hbm, positive_hbm, powers_ref, mixed_ref, total_ref, smooth_ref,
             query_t_ref, query_ref, positive_ref, page, positives, sems, stats):
    page_copy = pltpu.make_async_copy(page_hbm, page, sems.at[0])
    query_copy = pltpu.make_async_copy(query_hbm, query_ref, sems.at[1])
    positive_copy = pltpu.make_async_copy(positive_hbm, positives, sems.at[2])
    page_copy.start()
    query_copy.start()
    positive_copy.start()
    positive_copy.wait()
    token, query = of_token((positives.shape[1], query_ref.shape[0]), 1, tokens)
    inside = (token >= query * tokens) & (token < query * tokens + tokens)
    positive_ref[...] = jnp.sum(jnp.where(inside, positives[...].astype(jnp.float32).T, 0.0), axis=0, keepdims=True)
    page_copy.wait()
    query_copy.wait()
    token_powers(page, query_ref, powers_ref, stats, 0)
    smooth_ref[...] = token_rows(stats, 1, total_ref)[0]
    mix_pages(page, powers_ref, mixed_ref)
    query_t_ref[...] = turned(query_ref[...])


def far_body(page, query, powers_ref, total_ref, smooth_ref, stats):
    token_powers(page, query, powers_ref, stats, 0)
    smooth_ref[...] = token_rows(stats, 1, total_ref)[0]


def query_sums(value, tokens):
    parts = []
    for start in range(0, value.shape[1], LANES):
        part = value[:, start : start + LANES]
        lane = lax.broadcasted_iota(jnp.int32, part.shape, 1)
        step = tokens // 2
        while step:
            ahead = pltpu.roll(part, LANES - step, 1)
            behind = pltpu.roll(part, step, 1)
            part = part + jnp.where((lane & step) != 0, behind, ahead)
            step //= 2
        parts.append(part)
    return jnp.concatenate(parts, axis=1)


def mate_body(page, query, smooth_c, powers_ref, total_ref, smooth_ref, stats):
    token_powers(page, query, powers_ref, stats, 0)
    smooth_ref[0:1, :] = smooth_c[...]
    smooth_ref[1:2, :] = token_rows(stats, 1, total_ref)[0]


def last_body(tokens, page, mate_query, smooth_a, smooth_far, positive,
              powers_ref, total_ref, message_ref, stats):
    token_powers(page, mate_query, powers_ref, stats, 0)
    smooth = token_rows(stats, 1, total_ref)
    sums = query_sums(jnp.concatenate([smooth_a[...], smooth_far[...]] + smooth, axis=0), tokens)
    message_ref[0:4, :] = sums
    message_ref[4:5, :] = positive[...]
    message_ref[5:8, :] = sums[0:3, :]


def mix_body(far_page, mate_query, powers_c, powers_d, mixed_c_ref, mixed_d_ref, mate_query_t_ref):
    mate_query_t_ref[...] = turned(mate_query[...])
    mix_pages(far_page, powers_c, mixed_c_ref)
    mix_pages(far_page, powers_d, mixed_d_ref)


def loss_of(scores, positive):
    flags = [(positive == float(offset)).astype(jnp.float32) for offset in range(4)]
    positive_score = sum(flag * score for flag, score in zip(flags, scores))
    return sum((1.0 - flag) * jax.nn.softplus(score - positive_score) for flag, score in zip(flags, scores))


def slopes_of(scores, positive):
    flags = [(positive == float(offset)).astype(jnp.float32) for offset in range(4)]
    positive_score = sum(flag * score for flag, score in zip(flags, scores))
    margins = [score - positive_score for score in scores]
    terms = [(1.0 - flag) * jax.nn.sigmoid(margin) for flag, margin in zip(flags, margins)]
    total = sum(terms)
    return [term - flag * total for flag, term in zip(flags, terms)]


def to_short(value):
    largest = jnp.maximum(jnp.max(jnp.abs(value), axis=0, keepdims=True), 1e-38)
    power = jnp.minimum(jnp.floor(math.log2(32000.0) - jnp.log2(largest)), 126.0)
    short = jnp.round(value * jnp.exp2(power)).astype(jnp.int32).astype(jnp.int16)
    tail = jnp.broadcast_to(power, (PAD, value.shape[1])).astype(jnp.int32).astype(jnp.int16)
    return short, tail


def from_short(ref, rows):
    power = ref[rows : rows + PAD, :].astype(jnp.int32).astype(jnp.float32)[0:1, :]
    return ref[0:rows, :].astype(jnp.int32).astype(jnp.float32) * jnp.exp2(-power)


def scaled(query_t, weight):
    return (query_t.astype(jnp.float32) * weight).astype(jnp.bfloat16)


def put_short(ref, value):
    count = value.shape[0]
    short, tail = to_short(value)
    ref[0:count, :] = short
    for start in range(count, ref.shape[0], PAD):
        ref[start : start + PAD, :] = tail


def is_even():
    return lax.axis_index("dp") % 2 == 0


def own_scores(even, own, mate):
    return [own[0:1], jnp.where(even, mate[2:3], mate[3:4]), own[1:2], jnp.where(even, mate[3:4], mate[2:3])]


def send_far_body(message, arrived, total_a, total_c, total_d, total_b, query_t, mate_query_t, powers_c, powers_d,
                  out_ref, weight_ref):
    even = is_even()
    own = message[...]
    mate = arrived[...]
    slopes = slopes_of(own_scores(even, own, mate), own[4:5])
    mate_slopes = slopes_of(
        [mate[0:1], jnp.where(even, own[3:4], own[2:3]), mate[1:2], jnp.where(even, own[2:3], own[3:4])], mate[4:5])
    weight_c = slopes[2] / total_c[...]
    weight_d = jnp.where(even, mate_slopes[3], mate_slopes[1]) / total_d[...]
    weight_ref[0:1, :] = slopes[0] / total_a[...]
    weight_ref[1:2, :] = jnp.where(even, mate_slopes[1], mate_slopes[3]) / total_b[...]
    weight_ref[2:3, :] = weight_c
    weight_ref[3:4, :] = weight_d
    term = page_terms(query_t, weight_c, powers_c) + page_terms(mate_query_t, weight_d, powers_d)
    put_short(out_ref, term.T)


def send_last_body(weight, mate_query_t, powers_b, out_ref):
    put_short(out_ref, page_terms(mate_query_t, weight[1:2, :], powers_b).T)


def send_query_body(tokens, weight, last_page, powers_b, mixed_d, message, arrived, out_ref, loss_ref):
    own = message[...]
    loss = loss_of(own_scores(is_even(), own, arrived[...]), own[4:5])
    mixed_b = jnp.dot(powers_b[...], last_page[...], preferred_element_type=jnp.float32)
    columns = weight_columns(weight)
    put_short(out_ref, mixed_b * columns[:, 1:2] + mixed_d[...] * columns[:, 3:4])
    token, query = of_token((loss_ref.shape[1], loss.shape[1]), 1, tokens)
    loss_ref[...] = jnp.sum(jnp.where(token == query * tokens, loss, 0.0), axis=1, keepdims=True).T


def keep_body(weight, query_t, powers_a, mixed_a, mixed_c, page_ref, query_ref):
    columns = weight_columns(weight)
    page_ref[...] = page_terms(query_t, weight[0:1, :], powers_a).T
    query_ref[...] = mixed_a[...] * columns[:, 0:1] + mixed_c[...] * columns[:, 2:3]


def sum_body(own, *refs):
    total = own[...]
    for arrived in refs[:-1]:
        total = total + from_short(arrived, own.shape[0])
    refs[-1][...] = total


def last_sums_body(query_own, query_in, loss_row, page_own, last_in, far_in, query_ref, loss_ref, page_ref):
    sum_body(query_own, query_in, query_ref)
    loss_ref[...] = loss_row[0, :]
    sum_body(page_own, far_in, last_in, page_ref)


def last_sums(query_own, query_in, loss_row, page_own, last_in, far_in):
    shapes = (query_own.shape, loss_row.shape[1:], page_own.shape)
    return pl.pallas_call(
        last_sums_body,
        out_shape=[jax.ShapeDtypeStruct(shape, jnp.float32) for shape in shapes],
        in_specs=[VMEM] * 6,
        out_specs=[VMEM] * 3,
        compiler_params=pltpu.CompilerParams(vmem_limit_bytes=4 * MIB),
        cost_estimate=pl.CostEstimate(flops=1000, bytes_accessed=1000, transcendentals=0),
        name="last_sums",
    )(query_own, query_in, loss_row, page_own, last_in, far_in)


def in_hbm(value):
    return pltpu.with_memory_space_constraint(value, pltpu.HBM)


def on_device(queries, positives, pages):
    count, tokens, width = queries.shape
    page = pages[0]
    patches = page.shape[0]
    query = queries.reshape(count * tokens, width)
    rows = count * tokens
    f32, bf16, i16 = jnp.float32, jnp.bfloat16, jnp.int16
    unit = 2 * rows * patches * width

    far_page = passed_along(page, "dp", 2)
    last_page = odd_passed_along(page, "dp", 4)
    mate_query = swapped(query, "dp")

    powers_a, mixed_a, total_a, smooth_a, query_t, own_query, positive = on_core(
        functools.partial(own_body, tokens),
        [((rows, patches), bf16), ((rows, width), f32), ((1, rows), f32), ((1, rows), f32), ((width, rows), bf16),
         ((rows, width), bf16), ((1, rows), f32)],
        tuple(in_hbm(value) for value in (page, query, positives[None])), 2 * unit, "own_unit", specs=[ANY] * 3,
        scratch=[pltpu.VMEM((patches, width), bf16), pltpu.VMEM((1, count), jnp.int32), pltpu.SemaphoreType.DMA((3,)),
                 pltpu.VMEM((rows, COLUMNS), f32)])
    powers_c, total_c, smooth_c = on_core(
        far_body, [((rows, patches), bf16), ((1, rows), f32), ((1, rows), f32)], (far_page, own_query), unit, "far_unit",
        scratch=[pltpu.VMEM((rows, COLUMNS), f32)])
    powers_d, total_d, smooth_far = on_core(
        mate_body, [((rows, patches), bf16), ((1, rows), f32), ((2, rows), f32)],
        (far_page, mate_query, smooth_c), unit, "mate_unit",
        scratch=[pltpu.VMEM((rows, COLUMNS), f32)])
    powers_b, total_b, message = on_core(
        functools.partial(last_body, tokens),
        [((rows, patches), bf16), ((1, rows), f32), ((8, rows), f32)],
        (last_page, mate_query, smooth_a, smooth_far, positive), unit, "last_unit",
        scratch=[pltpu.VMEM((rows, COLUMNS), f32)])
    arrived = swapped(message, "dp")
    mixed_c, mixed_d, mate_query_t = on_core(
        mix_body, [((rows, width), f32)] * 2 + [((width, rows), bf16)],
        (far_page, mate_query, powers_c, powers_d), 2 * unit, "mixes")
    far_out, weight = on_core(
        send_far_body,
        [((patches + 4 * PAD, width), i16), ((4, rows), f32)],
        (message, arrived, total_a, total_c, total_d, total_b, query_t, mate_query_t, powers_c, powers_d),
        2 * unit, "send_far")
    far_in = passed_along(far_out, "dp", -2)
    last_out, = on_core(
        send_last_body, [((patches + 3 * PAD, width), i16)], (weight, mate_query_t, powers_b), unit, "send_last")
    last_in = odd_passed_along(last_out, "dp", -4)
    query_out, loss = on_core(
        functools.partial(send_query_body, tokens),
        [((rows + PAD, width), i16), ((1, count), f32)],
        (weight, last_page, powers_b, mixed_d, message, arrived), 1000, "send_query")
    query_in = swapped(query_out, "dp")
    page_own, query_own = on_core(
        keep_body, [((patches, width), f32), ((rows, width), f32)],
        (weight, query_t, powers_a, mixed_a, mixed_c), 1000, "own_terms")
    query_grad, loss, page_grad = last_sums(query_own, query_in, loss, page_own, last_in, far_in)
    return (loss, query_grad.reshape(count, tokens, width), page_grad[None])


def solution(mesh):
    in_specs = (P("dp", None, None), P("dp"), P("dp", None, None))
    out_specs = (P("dp"), P("dp", None, None), P("dp", None, None))
    return jax.shard_map(
        on_device, mesh=mesh, in_specs=in_specs, out_specs=out_specs, check_vma=False
    )
```

```python
import functools
import math

import jax
import jax.numpy as jnp
from jax import lax
from jax.experimental import pallas as pl
from jax.experimental.pallas import tpu as pltpu
from jax.sharding import PartitionSpec as P


tau_scale = 0.1
EXPONENT = math.log2(math.e) / tau_scale
CHUNK = 128
COLUMNS = 8
LANES = 128
PAD = 16
MIB = 1024 * 1024

VMEM = pl.BlockSpec(memory_space=pltpu.VMEM)
ANY = pl.BlockSpec(memory_space=pl.ANY)


def passed_along(value, axis, steps):
    count = lax.axis_size(axis)
    pairs = [(source, (source + steps) % count) for source in range(count)]
    return lax.ppermute(value, axis, pairs)


def odd_passed_along(value, axis, steps):
    count = lax.axis_size(axis)
    pairs = [(source, (source + steps) % count if source % 2 else source) for source in range(count)]
    return lax.ppermute(value, axis, pairs)


def swapped(value, axis):
    return lax.ppermute(value, axis, [(source, source ^ 1) for source in range(lax.axis_size(axis))])


def on_core(body, outs, args, flops, name, limit=8, specs=None, scratch=()):
    return pl.pallas_call(
        body,
        out_shape=[pltpu.VMEM(shape, dtype) for shape, dtype in outs],
        in_specs=specs or [VMEM] * len(args),
        out_specs=[VMEM] * len(outs),
        scratch_shapes=list(scratch),
        compiler_params=pltpu.CompilerParams(vmem_limit_bytes=limit * MIB),
        cost_estimate=pl.CostEstimate(flops=flops, bytes_accessed=2 * MIB, transcendentals=0),
        name=name,
    )(*args)


def rows_dot(a, b):
    return lax.dot_general(a, b, (((1,), (1,)), ((), ())), preferred_element_type=jnp.float32)


def token_powers(page, query, powers_ref, stats_ref, unit):
    rows = query.shape[0]
    for start in range(0, rows, CHUNK):
        cut = slice(start, start + CHUNK)
        products = rows_dot(query[cut, :], page[...])
        largest = jnp.max(products, axis=1, keepdims=True)
        powers = jnp.exp2((products - largest) * EXPONENT)
        powers_ref[cut, :] = powers.astype(jnp.bfloat16)
        stats_ref[cut, 2 * unit : 2 * unit + 1] = largest
        stats_ref[cut, 2 * unit + 1 : 2 * unit + 2] = jnp.sum(powers, axis=1, keepdims=True)


def token_rows(stats_ref, units, total_ref):
    stats = stats_ref[...].T
    smooth = []
    for unit in range(units):
        total = stats[2 * unit + 1 : 2 * unit + 2, :]
        total_ref[unit : unit + 1, :] = total
        smooth.append(stats[2 * unit : 2 * unit + 1, :] + tau_scale * jnp.log(total))
    return smooth


def mix_pages(page, powers_ref, mixed_ref):
    mixed_ref[...] = jnp.dot(powers_ref[...], page[...], preferred_element_type=jnp.float32)


def page_terms(query_t, weight, powers_ref):
    return jnp.dot(scaled(query_t[...], weight), powers_ref[...], preferred_element_type=jnp.float32)


def weight_columns(weight):
    return jnp.concatenate([weight[...], weight[...]], axis=0).T


def turned(value):
    return value.astype(jnp.float32).T.astype(jnp.bfloat16)


def of_token(shape, token_axis, tokens):
    token = lax.broadcasted_iota(jnp.int32, shape, token_axis)
    query = lax.broadcasted_iota(jnp.int32, shape, 1 - token_axis)
    return token, query


def own_body(tokens, page_hbm, query_hbm, positive_hbm, powers_ref, mixed_ref, total_ref, smooth_ref,
             query_t_ref, query_ref, positive_ref, page, positives, sems, stats):
    page_copy = pltpu.make_async_copy(page_hbm, page, sems.at[0])
    query_copy = pltpu.make_async_copy(query_hbm, query_ref, sems.at[1])
    positive_copy = pltpu.make_async_copy(positive_hbm, positives, sems.at[2])
    page_copy.start()
    query_copy.start()
    positive_copy.start()
    positive_copy.wait()
    token, query = of_token((positives.shape[1], query_ref.shape[0]), 1, tokens)
    inside = (token >= query * tokens) & (token < query * tokens + tokens)
    positive_ref[...] = jnp.sum(jnp.where(inside, positives[...].astype(jnp.float32).T, 0.0), axis=0, keepdims=True)
    page_copy.wait()
    query_copy.wait()
    token_powers(page, query_ref, powers_ref, stats, 0)
    smooth_ref[...] = token_rows(stats, 1, total_ref)[0]
    mix_pages(page, powers_ref, mixed_ref)
    query_t_ref[...] = turned(query_ref[...])


def far_body(page, query, powers_ref, total_ref, smooth_ref, stats):
    token_powers(page, query, powers_ref, stats, 0)
    smooth_ref[...] = token_rows(stats, 1, total_ref)[0]


def query_sums(value, tokens):
    parts = []
    for start in range(0, value.shape[1], LANES):
        part = value[:, start : start + LANES]
        lane = lax.broadcasted_iota(jnp.int32, part.shape, 1)
        step = tokens // 2
        while step:
            ahead = pltpu.roll(part, LANES - step, 1)
            behind = pltpu.roll(part, step, 1)
            part = part + jnp.where((lane & step) != 0, behind, ahead)
            step //= 2
        parts.append(part)
    return jnp.concatenate(parts, axis=1)


def mate_body(page, query, smooth_c, powers_ref, total_ref, smooth_ref, stats):
    token_powers(page, query, powers_ref, stats, 0)
    smooth_ref[0:1, :] = smooth_c[...]
    smooth_ref[1:2, :] = token_rows(stats, 1, total_ref)[0]


def last_body(tokens, page, mate_query, smooth_a, smooth_far, positive,
              powers_ref, total_ref, message_ref, stats):
    token_powers(page, mate_query, powers_ref, stats, 0)
    smooth = token_rows(stats, 1, total_ref)
    sums = query_sums(jnp.concatenate([smooth_a[...], smooth_far[...]] + smooth, axis=0), tokens)
    message_ref[0:4, :] = sums
    message_ref[4:5, :] = positive[...]
    message_ref[5:8, :] = sums[0:3, :]


def mix_body(far_page, last_page, mate_query, powers_d, powers_b, mixed_d_ref, mixed_b_ref, mate_query_t_ref):
    mate_query_t_ref[...] = turned(mate_query[...])
    mix_pages(far_page, powers_d, mixed_d_ref)
    mix_pages(last_page, powers_b, mixed_b_ref)


def loss_of(scores, positive):
    flags = [(positive == float(offset)).astype(jnp.float32) for offset in range(4)]
    positive_score = sum(flag * score for flag, score in zip(flags, scores))
    return sum((1.0 - flag) * jax.nn.softplus(score - positive_score) for flag, score in zip(flags, scores))


def slopes_of(scores, positive):
    flags = [(positive == float(offset)).astype(jnp.float32) for offset in range(4)]
    positive_score = sum(flag * score for flag, score in zip(flags, scores))
    margins = [score - positive_score for score in scores]
    terms = [(1.0 - flag) * jax.nn.sigmoid(margin) for flag, margin in zip(flags, margins)]
    total = sum(terms)
    return [term - flag * total for flag, term in zip(flags, terms)]


def to_short(value):
    largest = jnp.maximum(jnp.max(jnp.abs(value), axis=0, keepdims=True), 1e-38)
    power = jnp.minimum(jnp.floor(math.log2(32000.0) - jnp.log2(largest)), 126.0)
    short = jnp.round(value * jnp.exp2(power)).astype(jnp.int32).astype(jnp.int16)
    tail = jnp.broadcast_to(power, (PAD, value.shape[1])).astype(jnp.int32).astype(jnp.int16)
    return short, tail


def from_short(ref, rows):
    power = ref[rows : rows + PAD, :].astype(jnp.int32).astype(jnp.float32)[0:1, :]
    return ref[0:rows, :].astype(jnp.int32).astype(jnp.float32) * jnp.exp2(-power)


def scaled(query_t, weight):
    return (query_t.astype(jnp.float32) * weight).astype(jnp.bfloat16)


def put_short(ref, value):
    count = value.shape[0]
    short, tail = to_short(value)
    ref[0:count, :] = short
    for start in range(count, ref.shape[0], PAD):
        ref[start : start + PAD, :] = tail


def is_even():
    return lax.axis_index("dp") % 2 == 0


def own_scores(even, own, mate):
    return [own[0:1], jnp.where(even, mate[2:3], mate[3:4]), own[1:2], jnp.where(even, mate[3:4], mate[2:3])]


def send_far_body(message, arrived, total_a, total_c, total_d, total_b, query_t, mate_query_t, powers_c, powers_d,
                  out_ref, weight_ref):
    even = is_even()
    own = message[...]
    mate = arrived[...]
    slopes = slopes_of(own_scores(even, own, mate), own[4:5])
    mate_slopes = slopes_of(
        [mate[0:1], jnp.where(even, own[3:4], own[2:3]), mate[1:2], jnp.where(even, own[2:3], own[3:4])], mate[4:5])
    weight_c = slopes[2] / total_c[...]
    weight_d = jnp.where(even, mate_slopes[3], mate_slopes[1]) / total_d[...]
    weight_ref[0:1, :] = slopes[0] / total_a[...]
    weight_ref[1:2, :] = jnp.where(even, mate_slopes[1], mate_slopes[3]) / total_b[...]
    weight_ref[2:3, :] = weight_c
    weight_ref[3:4, :] = weight_d
    term = page_terms(query_t, weight_c, powers_c) + page_terms(mate_query_t, weight_d, powers_d)
    put_short(out_ref, term.T)


def send_last_body(weight, mate_query_t, powers_b, out_ref):
    put_short(out_ref, page_terms(mate_query_t, weight[1:2, :], powers_b).T)


def send_query_body(weight, mixed_b, mixed_d, out_ref):
    columns = weight_columns(weight)
    put_short(out_ref, mixed_b[...] * columns[:, 1:2] + mixed_d[...] * columns[:, 3:4])


def keep_body(tokens, weight, query_t, powers_a, mixed_a, far_page, powers_c, message, arrived,
              page_ref, query_ref, loss_ref):
    columns = weight_columns(weight)
    page_ref[...] = page_terms(query_t, weight[0:1, :], powers_a).T
    mixed_c = jnp.dot(powers_c[...], far_page[...], preferred_element_type=jnp.float32)
    query_ref[...] = mixed_a[...] * columns[:, 0:1] + mixed_c * columns[:, 2:3]
    own = message[...]
    loss = loss_of(own_scores(is_even(), own, arrived[...]), own[4:5])
    token, query = of_token((loss_ref.shape[1], loss.shape[1]), 1, tokens)
    loss_ref[...] = jnp.sum(jnp.where(token == query * tokens, loss, 0.0), axis=1, keepdims=True).T


def sum_body(own, *refs):
    total = own[...]
    for arrived in refs[:-1]:
        total = total + from_short(arrived, own.shape[0])
    refs[-1][...] = total


def last_sums_body(query_own, query_in, loss_row, page_own, last_in, far_in, query_ref, loss_ref, page_ref):
    sum_body(query_own, query_in, query_ref)
    loss_ref[...] = loss_row[0, :]
    sum_body(page_own, far_in, last_in, page_ref)


def last_sums(query_own, query_in, loss_row, page_own, last_in, far_in):
    shapes = (query_own.shape, loss_row.shape[1:], page_own.shape)
    return pl.pallas_call(
        last_sums_body,
        out_shape=[jax.ShapeDtypeStruct(shape, jnp.float32) for shape in shapes],
        in_specs=[VMEM] * 6,
        out_specs=[VMEM] * 3,
        compiler_params=pltpu.CompilerParams(vmem_limit_bytes=4 * MIB),
        cost_estimate=pl.CostEstimate(flops=1000, bytes_accessed=1000, transcendentals=0),
        name="last_sums",
    )(query_own, query_in, loss_row, page_own, last_in, far_in)


def in_hbm(value):
    return pltpu.with_memory_space_constraint(value, pltpu.HBM)


def on_device(queries, positives, pages):
    count, tokens, width = queries.shape
    page = pages[0]
    patches = page.shape[0]
    query = queries.reshape(count * tokens, width)
    rows = count * tokens
    f32, bf16, i16 = jnp.float32, jnp.bfloat16, jnp.int16
    unit = 2 * rows * patches * width

    far_page = passed_along(page, "dp", 2)
    last_page = odd_passed_along(page, "dp", 4)
    mate_query = swapped(query, "dp")

    powers_a, mixed_a, total_a, smooth_a, query_t, own_query, positive = on_core(
        functools.partial(own_body, tokens),
        [((rows, patches), bf16), ((rows, width), f32), ((1, rows), f32), ((1, rows), f32), ((width, rows), bf16),
         ((rows, width), bf16), ((1, rows), f32)],
        tuple(in_hbm(value) for value in (page, query, positives[None])), 2 * unit, "own_unit", specs=[ANY] * 3,
        scratch=[pltpu.VMEM((patches, width), bf16), pltpu.VMEM((1, count), jnp.int32), pltpu.SemaphoreType.DMA((3,)),
                 pltpu.VMEM((rows, COLUMNS), f32)])
    powers_c, total_c, smooth_c = on_core(
        far_body, [((rows, patches), bf16), ((1, rows), f32), ((1, rows), f32)], (far_page, own_query), unit, "far_unit",
        scratch=[pltpu.VMEM((rows, COLUMNS), f32)])
    powers_d, total_d, smooth_far = on_core(
        mate_body, [((rows, patches), bf16), ((1, rows), f32), ((2, rows), f32)],
        (far_page, mate_query, smooth_c), unit, "mate_unit",
        scratch=[pltpu.VMEM((rows, COLUMNS), f32)])
    powers_b, total_b, message = on_core(
        functools.partial(last_body, tokens),
        [((rows, patches), bf16), ((1, rows), f32), ((8, rows), f32)],
        (last_page, mate_query, smooth_a, smooth_far, positive), unit, "last_unit",
        scratch=[pltpu.VMEM((rows, COLUMNS), f32)])
    arrived = swapped(message, "dp")
    mixed_d, mixed_b, mate_query_t = on_core(
        mix_body, [((rows, width), f32)] * 2 + [((width, rows), bf16)],
        (far_page, last_page, mate_query, powers_d, powers_b), 2 * unit, "mixes")
    far_out, weight = on_core(
        send_far_body,
        [((patches + 4 * PAD, width), i16), ((4, rows), f32)],
        (message, arrived, total_a, total_c, total_d, total_b, query_t, mate_query_t, powers_c, powers_d),
        2 * unit, "send_far")
    far_in = passed_along(far_out, "dp", -2)
    last_out, = on_core(
        send_last_body, [((patches + 3 * PAD, width), i16)], (weight, mate_query_t, powers_b), unit, "send_last")
    last_in = odd_passed_along(last_out, "dp", -4)
    query_out, = on_core(
        send_query_body, [((rows + PAD, width), i16)], (weight, mixed_b, mixed_d), 1000, "send_query")
    query_in = swapped(query_out, "dp")
    page_own, query_own, loss = on_core(
        functools.partial(keep_body, tokens),
        [((patches, width), f32), ((rows, width), f32), ((1, count), f32)],
        (weight, query_t, powers_a, mixed_a, far_page, powers_c, message, arrived), 1000, "own_terms")
    query_grad, loss, page_grad = last_sums(query_own, query_in, loss, page_own, last_in, far_in)
    return (loss, query_grad.reshape(count, tokens, width), page_grad[None])


def solution(mesh):
    in_specs = (P("dp", None, None), P("dp"), P("dp", None, None))
    out_specs = (P("dp"), P("dp", None, None), P("dp", None, None))
    return jax.shard_map(
        on_device, mesh=mesh, in_specs=in_specs, out_specs=out_specs, check_vma=False
    )
```

```python
import functools
import math

import jax
import jax.numpy as jnp
from jax import lax
from jax.experimental import pallas as pl
from jax.experimental.pallas import tpu as pltpu
from jax.sharding import PartitionSpec as P


tau_scale = 0.1
EXPONENT = math.log2(math.e) / tau_scale
CHUNK = 128
COLUMNS = 8
LANES = 128
PAD = 16
MIB = 1024 * 1024

VMEM = pl.BlockSpec(memory_space=pltpu.VMEM)
ANY = pl.BlockSpec(memory_space=pl.ANY)


def passed_along(value, axis, steps):
    count = lax.axis_size(axis)
    pairs = [(source, (source + steps) % count) for source in range(count)]
    return lax.ppermute(value, axis, pairs)


def odd_passed_along(value, axis, steps):
    count = lax.axis_size(axis)
    pairs = [(source, (source + steps) % count if source % 2 else source) for source in range(count)]
    return lax.ppermute(value, axis, pairs)


def swapped(value, axis):
    return lax.ppermute(value, axis, [(source, source ^ 1) for source in range(lax.axis_size(axis))])


def on_core(body, outs, args, flops, name, limit=8, specs=None, scratch=()):
    return pl.pallas_call(
        body,
        out_shape=[pltpu.VMEM(shape, dtype) for shape, dtype in outs],
        in_specs=specs or [VMEM] * len(args),
        out_specs=[VMEM] * len(outs),
        scratch_shapes=list(scratch),
        compiler_params=pltpu.CompilerParams(vmem_limit_bytes=limit * MIB),
        cost_estimate=pl.CostEstimate(flops=flops, bytes_accessed=2 * MIB, transcendentals=0),
        name=name,
    )(*args)


def rows_dot(a, b):
    return lax.dot_general(a, b, (((1,), (1,)), ((), ())), preferred_element_type=jnp.float32)


def token_powers(page, query, powers_ref, stats_ref, unit):
    rows = query.shape[0]
    for start in range(0, rows, CHUNK):
        cut = slice(start, start + CHUNK)
        products = rows_dot(query[cut, :], page[...])
        largest = jnp.max(products, axis=1, keepdims=True)
        powers = jnp.exp2((products - largest) * EXPONENT)
        powers_ref[cut, :] = powers.astype(jnp.bfloat16)
        stats_ref[cut, 2 * unit : 2 * unit + 1] = largest
        stats_ref[cut, 2 * unit + 1 : 2 * unit + 2] = jnp.sum(powers, axis=1, keepdims=True)


def token_rows(stats_ref, units, total_ref):
    stats = stats_ref[...].T
    smooth = []
    for unit in range(units):
        total = stats[2 * unit + 1 : 2 * unit + 2, :]
        total_ref[unit : unit + 1, :] = total
        smooth.append(stats[2 * unit : 2 * unit + 1, :] + tau_scale * jnp.log(total))
    return smooth


def mix_pages(page, powers_ref, mixed_ref):
    mixed_ref[...] = jnp.dot(powers_ref[...], page[...], preferred_element_type=jnp.float32)


def page_terms(query_t, weight, powers_ref):
    return jnp.dot(scaled(query_t[...], weight), powers_ref[...], preferred_element_type=jnp.float32)


def weight_columns(weight):
    return jnp.concatenate([weight[...], weight[...]], axis=0).T


def turned(value):
    return value.astype(jnp.float32).T.astype(jnp.bfloat16)


def of_token(shape, token_axis, tokens):
    token = lax.broadcasted_iota(jnp.int32, shape, token_axis)
    query = lax.broadcasted_iota(jnp.int32, shape, 1 - token_axis)
    return token, query


def own_body(tokens, page_hbm, query_hbm, positive_hbm, powers_ref, mixed_ref, total_ref, smooth_ref,
             query_t_ref, query_ref, positive_ref, page, positives, sems, stats):
    page_copy = pltpu.make_async_copy(page_hbm, page, sems.at[0])
    query_copy = pltpu.make_async_copy(query_hbm, query_ref, sems.at[1])
    positive_copy = pltpu.make_async_copy(positive_hbm, positives, sems.at[2])
    page_copy.start()
    query_copy.start()
    positive_copy.start()
    positive_copy.wait()
    token, query = of_token((positives.shape[1], query_ref.shape[0]), 1, tokens)
    inside = (token >= query * tokens) & (token < query * tokens + tokens)
    positive_ref[...] = jnp.sum(jnp.where(inside, positives[...].astype(jnp.float32).T, 0.0), axis=0, keepdims=True)
    page_copy.wait()
    query_copy.wait()
    token_powers(page, query_ref, powers_ref, stats, 0)
    smooth_ref[...] = token_rows(stats, 1, total_ref)[0]
    mix_pages(page, powers_ref, mixed_ref)
    query_t_ref[...] = turned(query_ref[...])


def far_body(page, query, powers_ref, total_ref, smooth_ref, stats):
    token_powers(page, query, powers_ref, stats, 0)
    smooth_ref[...] = token_rows(stats, 1, total_ref)[0]


def query_sums(value, tokens):
    parts = []
    for start in range(0, value.shape[1], LANES):
        part = value[:, start : start + LANES]
        lane = lax.broadcasted_iota(jnp.int32, part.shape, 1)
        step = tokens // 2
        while step:
            ahead = pltpu.roll(part, LANES - step, 1)
            behind = pltpu.roll(part, step, 1)
            part = part + jnp.where((lane & step) != 0, behind, ahead)
            step //= 2
        parts.append(part)
    return jnp.concatenate(parts, axis=1)


def mate_body(page, query, smooth_c, powers_ref, total_ref, smooth_ref, mixed_ref, query_t_ref, stats):
    token_powers(page, query, powers_ref, stats, 0)
    query_t_ref[...] = turned(query[...])
    mix_pages(page, powers_ref, mixed_ref)
    smooth_ref[0:1, :] = smooth_c[...]
    smooth_ref[1:2, :] = token_rows(stats, 1, total_ref)[0]


def last_body(tokens, page, mate_query, smooth_a, smooth_far, positive,
              powers_ref, total_ref, message_ref, stats):
    token_powers(page, mate_query, powers_ref, stats, 0)
    smooth = token_rows(stats, 1, total_ref)
    sums = query_sums(jnp.concatenate([smooth_a[...], smooth_far[...]] + smooth, axis=0), tokens)
    message_ref[0:4, :] = sums
    message_ref[4:5, :] = positive[...]
    message_ref[5:8, :] = sums[0:3, :]


def last_mix_body(page, powers, total, mixed_ref, total_ref):
    mix_pages(page, powers, mixed_ref)
    total_ref[...] = total[...]


def loss_of(scores, positive):
    flags = [(positive == float(offset)).astype(jnp.float32) for offset in range(4)]
    positive_score = sum(flag * score for flag, score in zip(flags, scores))
    return sum((1.0 - flag) * jax.nn.softplus(score - positive_score) for flag, score in zip(flags, scores))


def slopes_of(scores, positive):
    flags = [(positive == float(offset)).astype(jnp.float32) for offset in range(4)]
    positive_score = sum(flag * score for flag, score in zip(flags, scores))
    margins = [score - positive_score for score in scores]
    terms = [(1.0 - flag) * jax.nn.sigmoid(margin) for flag, margin in zip(flags, margins)]
    total = sum(terms)
    return [term - flag * total for flag, term in zip(flags, terms)]


def to_short(value):
    largest = jnp.maximum(jnp.max(jnp.abs(value), axis=0, keepdims=True), 1e-38)
    power = jnp.minimum(jnp.floor(math.log2(32000.0) - jnp.log2(largest)), 126.0)
    short = jnp.round(value * jnp.exp2(power)).astype(jnp.int32).astype(jnp.int16)
    tail = jnp.broadcast_to(power, (PAD, value.shape[1])).astype(jnp.int32).astype(jnp.int16)
    return short, tail


def from_short(ref, rows):
    power = ref[rows : rows + PAD, :].astype(jnp.int32).astype(jnp.float32)[0:1, :]
    return ref[0:rows, :].astype(jnp.int32).astype(jnp.float32) * jnp.exp2(-power)


def scaled(query_t, weight):
    return (query_t.astype(jnp.float32) * weight).astype(jnp.bfloat16)


def put_short(ref, value):
    count = value.shape[0]
    short, tail = to_short(value)
    ref[0:count, :] = short
    for start in range(count, ref.shape[0], PAD):
        ref[start : start + PAD, :] = tail


def is_even():
    return lax.axis_index("dp") % 2 == 0


def own_scores(even, own, mate):
    return [own[0:1], jnp.where(even, mate[2:3], mate[3:4]), own[1:2], jnp.where(even, mate[3:4], mate[2:3])]


def send_far_body(message, arrived, total_a, total_c, total_d, total_b, query_t, mate_query_t, powers_c, powers_d,
                  out_ref, weight_ref):
    even = is_even()
    own = message[...]
    mate = arrived[...]
    slopes = slopes_of(own_scores(even, own, mate), own[4:5])
    mate_slopes = slopes_of(
        [mate[0:1], jnp.where(even, own[3:4], own[2:3]), mate[1:2], jnp.where(even, own[2:3], own[3:4])], mate[4:5])
    weight_c = slopes[2] / total_c[...]
    weight_d = jnp.where(even, mate_slopes[3], mate_slopes[1]) / total_d[...]
    weight_ref[0:1, :] = slopes[0] / total_a[...]
    weight_ref[1:2, :] = jnp.where(even, mate_slopes[1], mate_slopes[3]) / total_b[...]
    weight_ref[2:3, :] = weight_c
    weight_ref[3:4, :] = weight_d
    term = page_terms(query_t, weight_c, powers_c) + page_terms(mate_query_t, weight_d, powers_d)
    put_short(out_ref, term.T)


def send_last_body(weight, mate_query_t, powers_b, out_ref):
    put_short(out_ref, page_terms(mate_query_t, weight[1:2, :], powers_b).T)


def send_query_body(weight, mixed_b, mixed_d, out_ref):
    columns = weight_columns(weight)
    put_short(out_ref, mixed_b[...] * columns[:, 1:2] + mixed_d[...] * columns[:, 3:4])


def keep_body(tokens, weight, query_t, powers_a, mixed_a, far_page, powers_c, message, arrived,
              page_ref, query_ref, loss_ref):
    columns = weight_columns(weight)
    page_ref[...] = page_terms(query_t, weight[0:1, :], powers_a).T
    mixed_c = jnp.dot(powers_c[...], far_page[...], preferred_element_type=jnp.float32)
    query_ref[...] = mixed_a[...] * columns[:, 0:1] + mixed_c * columns[:, 2:3]
    own = message[...]
    loss = loss_of(own_scores(is_even(), own, arrived[...]), own[4:5])
    token, query = of_token((loss_ref.shape[1], loss.shape[1]), 1, tokens)
    loss_ref[...] = jnp.sum(jnp.where(token == query * tokens, loss, 0.0), axis=1, keepdims=True).T


def sum_body(own, *refs):
    total = own[...]
    for arrived in refs[:-1]:
        total = total + from_short(arrived, own.shape[0])
    refs[-1][...] = total


def last_sums_body(query_own, query_in, loss_row, page_own, last_in, far_in, query_ref, loss_ref, page_ref):
    sum_body(query_own, query_in, query_ref)
    loss_ref[...] = loss_row[0, :]
    sum_body(page_own, far_in, last_in, page_ref)


def last_sums(query_own, query_in, loss_row, page_own, last_in, far_in):
    shapes = (query_own.shape, loss_row.shape[1:], page_own.shape)
    return pl.pallas_call(
        last_sums_body,
        out_shape=[jax.ShapeDtypeStruct(shape, jnp.float32) for shape in shapes],
        in_specs=[VMEM] * 6,
        out_specs=[VMEM] * 3,
        compiler_params=pltpu.CompilerParams(vmem_limit_bytes=4 * MIB),
        cost_estimate=pl.CostEstimate(flops=1000, bytes_accessed=1000, transcendentals=0),
        name="last_sums",
    )(query_own, query_in, loss_row, page_own, last_in, far_in)


def in_hbm(value):
    return pltpu.with_memory_space_constraint(value, pltpu.HBM)


def on_device(queries, positives, pages):
    count, tokens, width = queries.shape
    page = pages[0]
    patches = page.shape[0]
    query = queries.reshape(count * tokens, width)
    rows = count * tokens
    f32, bf16, i16 = jnp.float32, jnp.bfloat16, jnp.int16
    unit = 2 * rows * patches * width

    far_page = passed_along(page, "dp", 2)
    last_page = odd_passed_along(page, "dp", 4)
    mate_query = swapped(query, "dp")

    powers_a, mixed_a, total_a, smooth_a, query_t, own_query, positive = on_core(
        functools.partial(own_body, tokens),
        [((rows, patches), bf16), ((rows, width), f32), ((1, rows), f32), ((1, rows), f32), ((width, rows), bf16),
         ((rows, width), bf16), ((1, rows), f32)],
        tuple(in_hbm(value) for value in (page, query, positives[None])), 2 * unit, "own_unit", specs=[ANY] * 3,
        scratch=[pltpu.VMEM((patches, width), bf16), pltpu.VMEM((1, count), jnp.int32), pltpu.SemaphoreType.DMA((3,)),
                 pltpu.VMEM((rows, COLUMNS), f32)])
    powers_c, total_c, smooth_c = on_core(
        far_body, [((rows, patches), bf16), ((1, rows), f32), ((1, rows), f32)], (far_page, own_query), unit, "far_unit",
        scratch=[pltpu.VMEM((rows, COLUMNS), f32)])
    powers_d, total_d, smooth_far, mixed_d, mate_query_t = on_core(
        mate_body,
        [((rows, patches), bf16), ((1, rows), f32), ((2, rows), f32), ((rows, width), f32), ((width, rows), bf16)],
        (far_page, mate_query, smooth_c), unit, "mate_unit",
        scratch=[pltpu.VMEM((rows, COLUMNS), f32)])
    powers_b, total_b, message = on_core(
        functools.partial(last_body, tokens),
        [((rows, patches), bf16), ((1, rows), f32), ((8, rows), f32)],
        (last_page, mate_query, smooth_a, smooth_far, positive), unit, "last_unit",
        scratch=[pltpu.VMEM((rows, COLUMNS), f32)])
    arrived = swapped(message, "dp")
    mixed_b, total_b = on_core(
        last_mix_body, [((rows, width), f32), ((1, rows), f32)], (last_page, powers_b, total_b), 2 * unit, "last_mix")
    far_out, weight = on_core(
        send_far_body,
        [((patches + 3 * PAD, width), i16), ((4, rows), f32)],
        (message, arrived, total_a, total_c, total_d, total_b, query_t, mate_query_t, powers_c, powers_d),
        2 * unit, "send_far")
    far_in = passed_along(far_out, "dp", -2)
    last_out, = on_core(
        send_last_body, [((patches + 2 * PAD, width), i16)], (weight, mate_query_t, powers_b), unit, "send_last")
    last_in = odd_passed_along(last_out, "dp", -4)
    query_out, = on_core(
        send_query_body, [((rows + PAD, width), i16)], (weight, mixed_b, mixed_d), 1000, "send_query")
    query_in = swapped(query_out, "dp")
    page_own, query_own, loss = on_core(
        functools.partial(keep_body, tokens),
        [((patches, width), f32), ((rows, width), f32), ((1, count), f32)],
        (weight, query_t, powers_a, mixed_a, far_page, powers_c, message, arrived), 1000, "own_terms")
    query_grad, loss, page_grad = last_sums(query_own, query_in, loss, page_own, last_in, far_in)
    return (loss, query_grad.reshape(count, tokens, width), page_grad[None])


def solution(mesh):
    in_specs = (P("dp", None, None), P("dp"), P("dp", None, None))
    out_specs = (P("dp"), P("dp", None, None), P("dp", None, None))
    return jax.shard_map(
        on_device, mesh=mesh, in_specs=in_specs, out_specs=out_specs, check_vma=False
    )
```
